32 devices in a mesh: layer: 4 (over y, x), front: 8 (over z, core).
Axes of the slice: x: 2, y: 2, z: 4, core: 2. Of those that a mesh axis runs over, the one named last changes fastest.
Arguments:
- right_sides: float32 [4, 2, 4, 1024], P('layer', None, None, 'front'), may hold values from -6 to 6
- leaf_inverse: bfloat16 [4, 2, 1024, 128], P('layer', None, 'front'), may hold values from -0.375 to 0.375
- couple_above: bfloat16 [4, 2, 1024, 128], P('layer', None, 'front'), may hold values from -0.1875 to 0.1875
- couple_below: bfloat16 [4, 2, 1024, 128], P('layer', None, 'front'), may hold values from -0.1875 to 0.1875
- sep_gather: bfloat16 [4, 2, 5120, 1024], P('layer', None, None, 'front'), may hold values from -0.125 to 0.125
- sep_inverse: bfloat16 [4, 2, 5120, 5120], P('layer', None, 'front'), may hold values from -0.0625 to 0.0625
- sep_spread: bfloat16 [4, 2, 1024, 5120], P('layer', None, 'front'), may hold values from -0.0625 to 0.0625
- panel_owner: int32 [4, 8], P('layer'), may hold values from 0 to 7, each once within a row
Outputs:
- solution: float32 [4, 2, 4, 1024], P('layer', None, None, 'front')
The draws below stay inside these ranges and needn't reach their ends.
Inputs may be any that keep to these rules, and one draw needn't show every extreme that they name: Each row of panel_owner names every slot 0 to 7 once.
All inputs are finite; a program needn't handle non-finite values.
Results may differ from the reference program's by a relative error of at most 0.023.
Values may be sent and summed in bfloat16 or wider, within the bound.
No kernel may reach another device: no remote copies, remote signals or barrier semaphores. Data moves between devices by JAX's collectives and lax.ppermute only.
A program may use at most 128 MiB of HBM per device.

```python
import jax
import jax.numpy as jnp

CELLS_DEV = 128
SEP = 5120
RHS = 4
LAYERS = 4
CELLS = 1024
N_LAYER = 4
N_FRONT = 8


def block_scale(rng, extent, split, least, top_value):
    level, own = 1.0, jax.random.fold_in(rng, 6)
    for axis_at, shards_of in split:
        steps = jnp.exp(jax.random.uniform(jax.random.fold_in(own, axis_at), (shards_of,), jnp.float32, least / len(split), top_value / len(split)))
        level = level * jnp.repeat(steps, extent[axis_at] // shards_of).reshape([-1 if axis == axis_at else 1 for axis in range(len(extent))])
    return level


def centred(key, shape, width, most, split=(), dtype=jnp.bfloat16):
    drawn = width * jax.random.normal(key, shape, jnp.float32)
    if split:
        drawn = drawn * block_scale(key, shape, split, -0.22, 0.18)
    return jnp.clip(drawn, -most, most).astype(dtype)


def setup_inputs(seed: int = 0) -> dict:
    key_list = jax.random.split(jax.random.key(seed), 9)
    return {
        "right_sides": centred(key_list[0], (LAYERS, 2, RHS, CELLS), 1.0, 6.0, ((0, 4), (3, 8)), jnp.float32),
        "leaf_inverse": centred(key_list[1], (LAYERS, 2, CELLS, CELLS_DEV), (2 * CELLS_DEV) ** -0.5, 0.375, ((0, 4), (2, 8))),
        "couple_above": centred(key_list[2], (LAYERS, 2, CELLS, CELLS_DEV), (8 * CELLS_DEV) ** -0.5, 0.1875, ((0, 4), (2, 8))),
        "couple_below": centred(key_list[3], (LAYERS, 2, CELLS, CELLS_DEV), (8 * CELLS_DEV) ** -0.5, 0.1875, ((0, 4), (2, 8))),
        "sep_gather": centred(key_list[4], (LAYERS, 2, SEP, CELLS), (2 * CELLS) ** -0.5, 0.125, ((0, 4), (3, 8))),
        "sep_inverse": centred(key_list[5], (LAYERS, 2, SEP, SEP), (2 * SEP) ** -0.5, 0.0625, ((0, 4), (2, 8))),
        "sep_spread": centred(key_list[6], (LAYERS, 2, CELLS, SEP), (2 * SEP) ** -0.5, 0.0625, ((0, 4), (2, 8))),
        "panel_owner": jax.vmap(lambda own: jax.random.permutation(own, N_FRONT))(jax.random.split(key_list[7], LAYERS)).reshape((LAYERS, N_FRONT)).astype(jnp.int32),
    }


def dense_apply(matrix, vector):
    def single(left, right):
        return jnp.dot(right, left.T, preferred_element_type=jnp.float32)
    real_part = single(matrix[0], vector[0]) - single(matrix[1], vector[1])
    imag_part = single(matrix[0], vector[1]) + single(matrix[1], vector[0])
    return jnp.stack([real_part, imag_part])


def block_apply(matrix, vector):
    blocks = matrix.astype(jnp.float32).reshape(2, -1, CELLS_DEV, CELLS_DEV)
    pieces = vector.astype(jnp.float32).reshape(2, RHS, -1, CELLS_DEV)

    def single(left, right):
        return jnp.einsum('nmk,rnk->rnm', left, right)
    real_part = single(blocks[0], pieces[0]) - single(blocks[1], pieces[1])
    imag_part = single(blocks[0], pieces[1]) + single(blocks[1], pieces[0])
    return jnp.stack([real_part, imag_part]).reshape(2, RHS, -1)


def layer_solve(source, leaf, gather_map, sep_matrix, spread):
    leaf_values = block_apply(leaf, source.astype(jnp.bfloat16))
    sep_sums = dense_apply(gather_map, leaf_values.astype(jnp.bfloat16))
    sep_values = dense_apply(sep_matrix, sep_sums.astype(jnp.bfloat16)).astype(jnp.bfloat16)
    return leaf_values - dense_apply(spread, sep_values)


def reference(right_sides, leaf_inverse, couple_above, couple_below, sep_gather, sep_inverse, sep_spread, panel_owner):
    ordered = []
    for level in range(N_LAYER):
        panels = sep_inverse[level].reshape(2, N_FRONT, SEP // N_FRONT, SEP)
        ordered.append(jnp.take(panels, panel_owner[level].astype(jnp.int32), axis=1).reshape(2, SEP, SEP))

    def solve(level, source):
        return layer_solve(source, leaf_inverse[level], sep_gather[level], ordered[level], sep_spread[level])

    forward = [solve(0, right_sides[0])]
    for level in range(1, N_LAYER):
        coupled = block_apply(couple_above[level], forward[level - 1].astype(jnp.bfloat16))
        forward.append(solve(level, right_sides[level] - coupled))
    solved = [None] * N_LAYER
    solved[N_LAYER - 1] = forward[N_LAYER - 1]
    for level in range(N_LAYER - 2, -1, -1):
        coupled = block_apply(couple_below[level], solved[level + 1].astype(jnp.bfloat16))
        solved[level] = forward[level] - solve(level, coupled)
    return jnp.stack(solved)
```

```python
import jax
import jax.numpy as jnp
from jax import lax
from jax.sharding import PartitionSpec as P


def xor_route(axis, distance):
    return [(i, i ^ distance) for i in range(lax.axis_size(axis))]


def pair(block):
    return lax.ppermute(block, "front", xor_route("front", 1))


FEW_CHIPS = 8


def same_core_groups():
    slots = lax.axis_size("front")
    return [list(range(core, slots, 2)) for core in range(2)]


def arrival_order(chip, chips):
    steps = jnp.arange(chips, dtype=jnp.int32)
    return chip ^ steps if chips <= FEW_CHIPS else steps


def gather_chips(block):
    chips = lax.axis_size("front") // 2
    if chips > FEW_CHIPS:
        return lax.all_gather(
            block, "front", axis=2, tiled=True, axis_index_groups=same_core_groups()
        )
    return jnp.concatenate(from_chips(block, chips), axis=2)


def sum_chips(block):
    chips = lax.axis_size("front") // 2
    if chips > FEW_CHIPS:
        return lax.psum(block, "front", axis_index_groups=same_core_groups())
    parts = from_chips(block.astype(jnp.bfloat16), chips)
    return sum(part.astype(jnp.float32) for part in parts)


def from_chips(block, chips):
    return [block] + [
        lax.ppermute(block, "front", xor_route("front", 2 * step)) for step in range(1, chips)
    ]


def combine(real_rows, imag_rows, count):
    real_part = real_rows[:count] - imag_rows[count:]
    imag_part = real_rows[count:] + imag_rows[:count]
    return jnp.stack([real_part, imag_part])


def dense_apply(matrix, vector):
    count = vector.shape[1]
    rows = vector.reshape(2 * count, vector.shape[2])
    both = lax.dot_general(
        rows, matrix, (((1,), (2,)), ((), ())), preferred_element_type=jnp.float32
    )
    return combine(both[:, 0], both[:, 1], count)


def block_apply(blocks, vector):
    size = blocks.shape[2]
    return jnp.concatenate(
        [dense_apply(blocks[:, i], vector[:, :, i * size : (i + 1) * size]) for i in range(2)],
        axis=2,
    )


def local(
    right_sides,
    leaf_inverse,
    couple_above,
    couple_below,
    sep_gather,
    sep_inverse,
    sep_spread,
    panel_owner,
):
    depth = lax.axis_size("layer")
    slots = lax.axis_size("front")
    chips = slots // 2
    layer = lax.axis_index("layer")
    place = lax.axis_index("front")
    core = place % 2
    sep = sep_inverse[0]
    cells = leaf_inverse.shape[2]
    total = sep_gather.shape[2]

    def with_partner(block, axis):
        return jnp.concatenate([block, pair(block)], axis=axis)

    halves = sep_gather[0].reshape(2, 2, total // 2, cells)
    own_half = lax.dynamic_index_in_dim(halves, core, 1, keepdims=False)
    other_half = lax.dynamic_index_in_dim(halves, 1 - core, 1, keepdims=False)
    gather_half = jnp.concatenate([own_half, pair(other_half)], axis=2)

    slot_ids = jnp.arange(slots, dtype=jnp.int32)
    panel_of = jnp.sum(
        jnp.where(panel_owner[0][None, :] == slot_ids[:, None], slot_ids[None, :], 0), axis=1
    )
    arrive = arrival_order(place // 2, chips)
    panels = sep_spread[0].reshape(2, cells, slots, total // slots)

    def columns(which):
        chosen = jnp.take(panels, panel_of[2 * arrive + which], axis=2)
        return chosen.reshape(2, cells, total // 2)

    spread_half = jnp.concatenate([columns(core), pair(columns(1 - core))], axis=1)

    leaf = jnp.stack([leaf_inverse[0], pair(leaf_inverse[0])], axis=1)
    above = jnp.stack([couple_above[0], pair(couple_above[0])], axis=1)
    below = jnp.stack([couple_below[0], pair(couple_below[0])], axis=1)
    sources = with_partner(right_sides[0], 2)

    def solve(source):
        leaf_values = block_apply(leaf, source.astype(jnp.bfloat16))
        partial_sums = dense_apply(gather_half, leaf_values.astype(jnp.bfloat16))
        half_sums = sum_chips(partial_sums).astype(jnp.bfloat16)
        other_sums = pair(half_sums)
        first = jnp.where(core == 0, half_sums, other_sums)
        second = jnp.where(core == 0, other_sums, half_sums)
        own_rows = dense_apply(sep, jnp.concatenate([first, second], axis=2)).astype(jnp.bfloat16)
        stored = gather_chips(own_rows)
        spread = dense_apply(spread_half, stored)
        theirs = pair(spread)
        spread = spread + jnp.concatenate([theirs[:, :, cells:], theirs[:, :, :cells]], axis=2)
        return leaf_values - spread

    def hop(value, source_layer, target_layer):
        return lax.ppermute(
            value.astype(jnp.bfloat16), "layer", xor_route("layer", source_layer ^ target_layer)
        )

    value = jnp.zeros_like(sources)
    value = lax.cond(layer == 0, lambda old: solve(sources), lambda old: old, value)
    for level in range(1, depth):
        arrived = hop(value, level - 1, level)
        value = lax.cond(
            layer == level,
            lambda old, got: solve(sources - block_apply(above, got)),
            lambda old, got: old,
            value,
            arrived,
        )
    for level in range(depth - 2, -1, -1):
        arrived = hop(value, level + 1, level)
        value = lax.cond(
            layer == level,
            lambda old, got: old - solve(block_apply(below, got)),
            lambda old, got: old,
            value,
            arrived,
        )
    return value[None, :, :, :cells]


def solution(mesh):
    return jax.shard_map(
        local,
        mesh=mesh,
        in_specs=(
            P("layer", None, None, "front"),
            P("layer", None, "front", None),
            P("layer", None, "front", None),
            P("layer", None, "front", None),
            P("layer", None, None, "front"),
            P("layer", None, "front", None),
            P("layer", None, "front", None),
            P("layer", None),
        ),
        out_specs=P("layer", None, None, "front"),
        check_vma=False,
    )
```

```python
import jax
import jax.numpy as jnp
from jax import lax
from jax.experimental import pallas as pl
from jax.experimental.pallas import tpu as pltpu
from jax.sharding import PartitionSpec as P

FEW_CHIPS = 8
BF16, F32 = jnp.bfloat16, jnp.float32
VMEM = pl.BlockSpec(memory_space=pltpu.VMEM)
MIB = 2**20


def xor_route(axis, distance):
    return [(i, i ^ distance) for i in range(lax.axis_size(axis))]


def pair(block):
    return lax.ppermute(block, "front", xor_route("front", 1))


def same_core_groups():
    slots = lax.axis_size("front")
    return [list(range(core, slots, 2)) for core in range(2)]


def arrival_order(chip, chips):
    steps = jnp.arange(chips, dtype=jnp.int32)
    return chip ^ steps if chips <= FEW_CHIPS else steps


def from_chips(block, chips):
    return [block] + [
        lax.ppermute(block, "front", xor_route("front", 2 * step)) for step in range(1, chips)
    ]


def gather_chips(block):
    chips = lax.axis_size("front") // 2
    if chips > FEW_CHIPS:
        groups = same_core_groups()
        return lax.all_gather(block, "front", axis=1, tiled=True, axis_index_groups=groups)
    return jnp.concatenate(from_chips(block, chips), axis=1)


def sum_chips(block):
    chips = lax.axis_size("front") // 2
    if chips > FEW_CHIPS:
        return lax.psum(block.astype(F32), "front", axis_index_groups=same_core_groups())
    return sum(part.astype(F32) for part in from_chips(block, chips))


def in_vmem(block):
    return pltpu.with_memory_space_constraint(block, pltpu.VMEM)


def params(mib):
    return pltpu.CompilerParams(vmem_limit_bytes=mib * MIB)


def cost(flops, nbytes):
    return pl.CostEstimate(flops=flops, bytes_accessed=nbytes, transcendentals=0)


def turned(vector):
    count = vector.shape[0] // 2
    return jnp.concatenate([-vector[count:], vector[:count]], axis=0)


def operands(vector):
    return vector.astype(BF16), turned(vector).astype(BF16)


def times(vector, real_matrix, imag_matrix, contract):
    straight, cross = operands(vector)
    dims = (((1,), (contract,)), ((), ()))
    return lax.dot_general(
        straight, real_matrix, dims, preferred_element_type=F32
    ) + lax.dot_general(cross, imag_matrix, dims, preferred_element_type=F32)


def transpose_sep(sep):
    _, rows, total = sep.shape
    step = 512

    def kernel(block, out):
        at = pl.multiple_of(pl.program_id(0) * step, step)
        for part in range(2):
            out[part, pl.ds(at, step), :] = block[part].T

    return pl.pallas_call(
        kernel,
        grid=(total // step,),
        in_specs=[pl.BlockSpec((2, rows, step), lambda i: (0, 0, i))],
        out_specs=VMEM,
        out_shape=pltpu.VMEM((2, total, rows), BF16),
        compiler_params=params(16),
        cost_estimate=cost(0, 4 * sep.size),
        name="transpose_sep",
    )(sep)


def transpose_gather(gather):
    _, total, cells = gather.shape
    half = total // 2
    step = 512

    def kernel(block, keep, give):
        core = lax.axis_index("front") % 2
        for out, start in ((keep, core * half), (give, (1 - core) * half)):
            for part in range(2):
                for at in range(0, half, step):
                    rows = pl.ds(pl.multiple_of(start + at, step), step)
                    out[part, :, pl.ds(at, step)] = block[part, rows, :].T

    shape = jax.ShapeDtypeStruct((2, cells, half), BF16)
    return pl.pallas_call(
        kernel,
        in_specs=[VMEM],
        out_specs=[VMEM, VMEM],
        out_shape=[shape, shape],
        compiler_params=params(16),
        cost_estimate=cost(0, 4 * gather.size),
        name="transpose_gather",
    )(gather)


def transpose_spread(spread, keep_panels, give_panels, rows):
    _, cells, total = spread.shape
    chips = keep_panels.shape[0]

    def kernel(order, keep_block, give_block, keep, give):
        for part in range(2):
            keep[part] = keep_block[part].T
            give[part] = give_block[part].T

    shape = jax.ShapeDtypeStruct((2, total // 2, cells), BF16)
    out_block = pl.BlockSpec((2, rows, cells), lambda i, order: (0, i, 0))
    return pl.pallas_call(
        kernel,
        grid_spec=pltpu.PrefetchScalarGridSpec(
            num_scalar_prefetch=1,
            grid=(chips,),
            in_specs=[
                pl.BlockSpec((2, cells, rows), lambda i, order: (0, 0, order[i])),
                pl.BlockSpec((2, cells, rows), lambda i, order: (0, 0, order[chips + i])),
            ],
            out_specs=[out_block, out_block],
        ),
        out_shape=[shape, shape],
        compiler_params=params(16),
        cost_estimate=cost(0, 4 * spread.size),
        name="transpose_spread",
    )(jnp.concatenate([keep_panels, give_panels]), spread, spread)


def join(keep, got, axis):
    shape = list(keep.shape)
    size = shape[axis]
    shape[axis] = 2 * size

    def kernel(keep_ref, got_ref, out):
        if axis == 1:
            out[:, :size, :] = keep_ref[...]
            out[:, size:, :] = got_ref[...]
        else:
            out[:, :, :size] = keep_ref[...]
            out[:, :, size:] = got_ref[...]

    return pl.pallas_call(
        kernel,
        in_specs=[VMEM, VMEM],
        out_specs=VMEM,
        out_shape=pltpu.VMEM(tuple(shape), BF16),
        compiler_params=params(16),
        cost_estimate=cost(0, 8 * keep.size),
        name="join",
    )(keep, got)


def leaf_and_gather(level, leaf, gather, sources=None, couple=None, arrived=None):
    cells = leaf[0].shape[1]
    width = gather.shape[2]
    given = [block for block in (arrived, sources) if block is not None]
    mats = list(couple or []) + list(leaf)

    def kernel(*refs):
        vectors = list(refs[: len(given)])
        matrices = list(refs[len(given) : len(given) + len(mats)])
        gather_ref, leaf_out, sums_out = refs[-3:]

        def blocks(vector, pair_of):
            return jnp.concatenate(
                [
                    times(vector[:, i * cells : (i + 1) * cells], pair_of[i][0], pair_of[i][1], 1)
                    for i in range(2)
                ],
                axis=1,
            )

        @pl.when(lax.axis_index("layer") == level)
        def _():
            if couple is None:
                source = vectors[0][...]
            else:
                source = blocks(vectors[0][...].astype(F32), matrices[:2])
                if sources is not None:
                    source = vectors[1][...] - source
            leaf_values = blocks(source, matrices[-2:])
            leaf_out[...] = leaf_values
            sums_out[...] = times(leaf_values, gather_ref[0], gather_ref[1], 0).astype(BF16)

    return pl.pallas_call(
        kernel,
        in_specs=[VMEM] * (len(given) + len(mats) + 1),
        out_specs=[VMEM, VMEM],
        out_shape=[
            jax.ShapeDtypeStruct((8, 2 * cells), F32),
            jax.ShapeDtypeStruct((8, width), BF16),
        ],
        compiler_params=params(16),
        cost_estimate=cost(32 * gather.size, 2 * gather.size),
        name="leaf_and_gather",
    )(*given, *mats, in_vmem(gather))


def sep_rows(level, sums, sep, other, before=None):
    half = sums.shape[1]
    rows = sep.shape[2]
    given = [sums] if before is None else [sums, before]

    def kernel(*refs):
        sums_ref, sep_ref, out = refs[0], refs[-2], refs[-1]

        @pl.when(lax.axis_index("layer") == level)
        def _():
            core = lax.axis_index("front") % 2
            side = 1 - core if other else core
            at = pl.ds(pl.multiple_of(side * half, half), half)
            value = times(sums_ref[...].astype(F32), sep_ref[0, at, :], sep_ref[1, at, :], 0)
            if before is not None:
                value = value + refs[1][...]
            out[...] = value.astype(out.dtype)

    return pl.pallas_call(
        kernel,
        in_specs=[VMEM] * (len(given) + 1),
        out_specs=VMEM,
        out_shape=jax.ShapeDtypeStruct((8, rows), F32 if before is None else BF16),
        compiler_params=params(16),
        cost_estimate=cost(16 * sep.size, sep.size),
        name="sep_rows",
    )(*given, in_vmem(sep))


def spread_cells(level, stored, spread):
    def kernel(stored_ref, spread_ref, out):
        @pl.when(lax.axis_index("layer") == level)
        def _():
            out[...] = times(stored_ref[...].astype(F32), spread_ref[0], spread_ref[1], 0)

    return pl.pallas_call(
        kernel,
        in_specs=[VMEM, VMEM],
        out_specs=VMEM,
        out_shape=jax.ShapeDtypeStruct((8, spread.shape[2]), F32),
        compiler_params=params(16),
        cost_estimate=cost(32 * spread.size, 2 * spread.size),
        name="spread_cells",
    )(stored, in_vmem(spread))


def local(
    right_sides,
    leaf_inverse,
    couple_above,
    couple_below,
    sep_gather,
    sep_inverse,
    sep_spread,
    panel_owner,
):
    depth = lax.axis_size("layer")
    slots = lax.axis_size("front")
    chips = slots // 2
    layer = lax.axis_index("layer")
    place = lax.axis_index("front")
    core = place % 2
    cells = leaf_inverse.shape[2]
    total = sep_gather.shape[2]
    rows = sep_inverse.shape[2]

    def with_partner(block):
        return [block, pair(block)]

    leaf = with_partner(leaf_inverse[0])
    sources = jnp.concatenate(with_partner(right_sides[0].reshape(8, cells)), axis=1)

    gather_keep, gather_give = transpose_gather(sep_gather[0])
    gather = join(gather_keep, pair(gather_give), 1)

    above = with_partner(couple_above[0])
    below = with_partner(couple_below[0])

    slot_ids = jnp.arange(slots, dtype=jnp.int32)
    panel_of = jnp.sum(
        jnp.where(panel_owner[0][None, :] == slot_ids[:, None], slot_ids[None, :], 0), axis=1
    )
    arrive = arrival_order(place // 2, chips)
    keep_panels, give_panels = panel_of[2 * arrive + core], panel_of[2 * arrive + 1 - core]
    if rows % 128 == 0:
        spread_keep, spread_give = transpose_spread(sep_spread[0], keep_panels, give_panels, rows)
    else:
        panels = sep_spread[0].reshape(2, cells, slots, rows)
        spread_keep, spread_give = (
            jnp.swapaxes(jnp.take(panels, which, axis=2).reshape(2, cells, total // 2), 1, 2)
            for which in (keep_panels, give_panels)
        )
    spread = join(spread_keep, pair(spread_give), 2)

    sep = transpose_sep(sep_inverse[0])

    def solve(level, **given):
        leaf_values, sums = leaf_and_gather(level, leaf, gather, **given)
        half_sums = sum_chips(sums).astype(BF16)
        other_sums = pair(half_sums)
        own_rows = sep_rows(level, half_sums, sep, False)
        own_rows = sep_rows(level, other_sums, sep, True, own_rows)
        part = spread_cells(level, gather_chips(own_rows), spread)
        theirs = pair(part)
        part = part + jnp.concatenate([theirs[:, cells:], theirs[:, :cells]], axis=1)
        return leaf_values - part

    def hop(value, source_layer, target_layer):
        route = xor_route("layer", source_layer ^ target_layer)
        return lax.ppermute(value.astype(BF16), "layer", route)

    value = solve(0, sources=sources)
    for level in range(1, depth):
        arrived = hop(value, level - 1, level)
        solved = solve(level, sources=sources, couple=above, arrived=arrived)
        value = jnp.where(layer == level, solved, value)
    for level in range(depth - 2, -1, -1):
        arrived = hop(value, level + 1, level)
        solved = solve(level, couple=below, arrived=arrived)
        value = jnp.where(layer == level, value - solved, value)
    return value[:, :cells].reshape(1, 2, 4, cells)


def solution(mesh):
    return jax.shard_map(
        local,
        mesh=mesh,
        in_specs=(
            P("layer", None, None, "front"),
            P("layer", None, "front", None),
            P("layer", None, "front", None),
            P("layer", None, "front", None),
            P("layer", None, None, "front"),
            P("layer", None, "front", None),
            P("layer", None, "front", None),
            P("layer", None),
        ),
        out_specs=P("layer", None, None, "front"),
        check_vma=False,
    )
```

```python
import jax
import jax.numpy as jnp
from jax import lax
from jax.experimental import pallas as pl
from jax.experimental.pallas import tpu as pltpu
from jax.sharding import PartitionSpec as P

FEW_CHIPS = 8
BF16, F32 = jnp.bfloat16, jnp.float32
VMEM = pl.BlockSpec(memory_space=pltpu.VMEM)
MIB = 2**20


def xor_route(axis, distance):
    return [(i, i ^ distance) for i in range(lax.axis_size(axis))]


def pair(block):
    return lax.ppermute(block, "front", xor_route("front", 1))


def same_core_groups():
    slots = lax.axis_size("front")
    return [list(range(core, slots, 2)) for core in range(2)]


def arrival_order(chip, chips):
    steps = jnp.arange(chips, dtype=jnp.int32)
    return chip ^ steps if chips <= FEW_CHIPS else steps


def from_chips(block, chips):
    return [block] + [
        lax.ppermute(block, "front", xor_route("front", 2 * step)) for step in range(1, chips)
    ]


def gather_chips(block):
    chips = lax.axis_size("front") // 2
    if chips > FEW_CHIPS:
        groups = same_core_groups()
        return lax.all_gather(block, "front", axis=1, tiled=True, axis_index_groups=groups)
    return jnp.concatenate(from_chips(block, chips), axis=1)


def sum_chips(block):
    chips = lax.axis_size("front") // 2
    if chips > FEW_CHIPS:
        return lax.psum(block.astype(F32), "front", axis_index_groups=same_core_groups())
    return sum(part.astype(F32) for part in from_chips(block, chips))


def in_vmem(block):
    return pltpu.with_memory_space_constraint(block, pltpu.VMEM)


def params(mib):
    return pltpu.CompilerParams(vmem_limit_bytes=mib * MIB)


def cost(flops, nbytes):
    return pl.CostEstimate(flops=flops, bytes_accessed=nbytes, transcendentals=0)


def turned(vector):
    count = vector.shape[0] // 2
    return jnp.concatenate([-vector[count:], vector[:count]], axis=0)


def operands(vector):
    return vector.astype(BF16), turned(vector).astype(BF16)


def times(vector, real_matrix, imag_matrix, contract):
    straight, cross = operands(vector)
    dims = (((1,), (contract,)), ((), ()))
    return lax.dot_general(
        straight, real_matrix, dims, preferred_element_type=F32
    ) + lax.dot_general(cross, imag_matrix, dims, preferred_element_type=F32)


def transpose_sep(sep):
    _, rows, total = sep.shape
    step = 512

    def kernel(block, out):
        at = pl.multiple_of(pl.program_id(0) * step, step)
        for part in range(2):
            out[part, pl.ds(at, step), :] = block[part].T

    return pl.pallas_call(
        kernel,
        grid=(total // step,),
        in_specs=[pl.BlockSpec((2, rows, step), lambda i: (0, 0, i))],
        out_specs=VMEM,
        out_shape=pltpu.VMEM((2, total, rows), BF16),
        compiler_params=params(16),
        cost_estimate=cost(0, 4 * sep.size),
        name="transpose_sep",
    )(sep)


def transpose_gather(gather):
    _, total, cells = gather.shape
    half = total // 2
    step = 512

    def kernel(block, keep, give):
        core = lax.axis_index("front") % 2
        for out, start in ((keep, core * half), (give, (1 - core) * half)):
            for part in range(2):
                for at in range(0, half, step):
                    rows = pl.ds(pl.multiple_of(start + at, step), step)
                    out[part, :, pl.ds(at, step)] = block[part, rows, :].T

    shape = jax.ShapeDtypeStruct((2, cells, half), BF16)
    return pl.pallas_call(
        kernel,
        in_specs=[VMEM],
        out_specs=[VMEM, VMEM],
        out_shape=[shape, shape],
        compiler_params=params(16),
        cost_estimate=cost(0, 4 * gather.size),
        name="transpose_gather",
    )(gather)


def transpose_spread(spread, keep_panels, give_panels, rows):
    _, cells, total = spread.shape
    chips = keep_panels.shape[0]

    def kernel(order, keep_block, give_block, keep, give):
        for part in range(2):
            keep[part] = keep_block[part].T
            give[part] = give_block[part].T

    shape = jax.ShapeDtypeStruct((2, total // 2, cells), BF16)
    out_block = pl.BlockSpec((2, rows, cells), lambda i, order: (0, i, 0))
    return pl.pallas_call(
        kernel,
        grid_spec=pltpu.PrefetchScalarGridSpec(
            num_scalar_prefetch=1,
            grid=(chips,),
            in_specs=[
                pl.BlockSpec((2, cells, rows), lambda i, order: (0, 0, order[i])),
                pl.BlockSpec((2, cells, rows), lambda i, order: (0, 0, order[chips + i])),
            ],
            out_specs=[out_block, out_block],
        ),
        out_shape=[shape, shape],
        compiler_params=params(16),
        cost_estimate=cost(0, 4 * spread.size),
        name="transpose_spread",
    )(jnp.concatenate([keep_panels, give_panels]), spread, spread)


def join(keep, got, axis):
    shape = list(keep.shape)
    size = shape[axis]
    shape[axis] = 2 * size

    def kernel(keep_ref, got_ref, out):
        if axis == 1:
            out[:, :size, :] = keep_ref[...]
            out[:, size:, :] = got_ref[...]
        else:
            out[:, :, :size] = keep_ref[...]
            out[:, :, size:] = got_ref[...]

    return pl.pallas_call(
        kernel,
        in_specs=[VMEM, VMEM],
        out_specs=VMEM,
        out_shape=pltpu.VMEM(tuple(shape), BF16),
        compiler_params=params(16),
        cost_estimate=cost(0, 8 * keep.size),
        name="join",
    )(keep, got)


def leaf_and_gather(level, leaf, gather, sources=None, couple=None, arrived=None):
    cells = leaf[0].shape[1]
    width = gather.shape[2]
    given = [block for block in (arrived, sources) if block is not None]
    mats = list(couple or []) + list(leaf)

    def kernel(*refs):
        vectors = list(refs[: len(given)])
        matrices = list(refs[len(given) : len(given) + len(mats)])
        gather_ref, leaf_out, sums_out = refs[-3:]

        def blocks(vector, pair_of):
            return jnp.concatenate(
                [
                    times(vector[:, i * cells : (i + 1) * cells], pair_of[i][0], pair_of[i][1], 1)
                    for i in range(2)
                ],
                axis=1,
            )

        @pl.when(lax.axis_index("layer") == level)
        def _():
            if couple is None:
                source = vectors[0][...]
            else:
                source = blocks(vectors[0][...].astype(F32), matrices[:2])
                if sources is not None:
                    source = vectors[1][...] - source
            leaf_values = blocks(source, matrices[-2:])
            leaf_out[...] = leaf_values
            sums_out[...] = times(leaf_values, gather_ref[0], gather_ref[1], 0).astype(BF16)

    return pl.pallas_call(
        kernel,
        in_specs=[VMEM] * (len(given) + len(mats) + 1),
        out_specs=[VMEM, VMEM],
        out_shape=[
            jax.ShapeDtypeStruct((8, 2 * cells), F32),
            jax.ShapeDtypeStruct((8, width), BF16),
        ],
        compiler_params=params(16),
        cost_estimate=cost(32 * gather.size, 2 * gather.size),
        name="leaf_and_gather",
    )(*given, *mats, in_vmem(gather))


def sep_rows(level, sums, sep, other, before=None):
    half = sums.shape[1]
    rows = sep.shape[2]
    given = [sums] if before is None else [sums, before]

    def kernel(*refs):
        sums_ref, sep_ref, out = refs[0], refs[-2], refs[-1]

        @pl.when(lax.axis_index("layer") == level)
        def _():
            core = lax.axis_index("front") % 2
            side = 1 - core if other else core
            at = pl.ds(pl.multiple_of(side * half, half), half)
            value = times(sums_ref[...].astype(F32), sep_ref[0, at, :], sep_ref[1, at, :], 0)
            if before is not None:
                value = value + refs[1][...]
            out[...] = value.astype(out.dtype)

    return pl.pallas_call(
        kernel,
        in_specs=[VMEM] * (len(given) + 1),
        out_specs=VMEM,
        out_shape=jax.ShapeDtypeStruct((8, rows), F32 if before is None else BF16),
        compiler_params=params(16),
        cost_estimate=cost(16 * sep.size, sep.size),
        name="sep_rows",
    )(*given, in_vmem(sep))


def spread_cells(level, stored, spread):
    def kernel(stored_ref, spread_ref, out):
        @pl.when(lax.axis_index("layer") == level)
        def _():
            out[...] = times(stored_ref[...].astype(F32), spread_ref[0], spread_ref[1], 0)

    return pl.pallas_call(
        kernel,
        in_specs=[VMEM, VMEM],
        out_specs=VMEM,
        out_shape=jax.ShapeDtypeStruct((8, spread.shape[2]), F32),
        compiler_params=params(16),
        cost_estimate=cost(32 * spread.size, 2 * spread.size),
        name="spread_cells",
    )(stored, in_vmem(spread))


def finish(level, leaf_values, part, theirs, before=None, subtract=False):
    cells = part.shape[1] // 2
    given = [leaf_values, part, theirs] + ([] if before is None else [before])

    def kernel(*refs):
        leaf_ref, part_ref, theirs_ref = refs[:3]
        value_out, sent_out = refs[-2:]
        here = lax.axis_index("layer") == level

        @pl.when(here)
        def _():
            swapped = jnp.concatenate([theirs_ref[:, cells:], theirs_ref[:, :cells]], axis=1)
            solved = leaf_ref[...] - (part_ref[...] + swapped)
            if subtract:
                solved = refs[3][...] - solved
            value_out[...] = solved
            sent_out[...] = solved.astype(BF16)

        if before is not None:

            @pl.when(jnp.logical_not(here))
            def _():
                value_out[...] = refs[3][...]
                sent_out[...] = refs[3][...].astype(BF16)

    return pl.pallas_call(
        kernel,
        in_specs=[VMEM] * len(given),
        out_specs=[VMEM, VMEM],
        out_shape=[
            jax.ShapeDtypeStruct(part.shape, F32),
            jax.ShapeDtypeStruct(part.shape, BF16),
        ],
        compiler_params=params(16),
        cost_estimate=cost(4 * part.size, 16 * part.size),
        name="finish",
    )(*given)


def local(
    right_sides,
    leaf_inverse,
    couple_above,
    couple_below,
    sep_gather,
    sep_inverse,
    sep_spread,
    panel_owner,
):
    depth = lax.axis_size("layer")
    slots = lax.axis_size("front")
    chips = slots // 2
    place = lax.axis_index("front")
    core = place % 2
    cells = leaf_inverse.shape[2]
    total = sep_gather.shape[2]
    rows = sep_inverse.shape[2]

    def with_partner(block):
        return [block, pair(block)]

    leaf = with_partner(leaf_inverse[0])
    sources = jnp.concatenate(with_partner(right_sides[0].reshape(8, cells)), axis=1)

    gather_keep, gather_give = transpose_gather(sep_gather[0])
    gather = join(gather_keep, pair(gather_give), 1)

    above = with_partner(couple_above[0])
    below = with_partner(couple_below[0])

    slot_ids = jnp.arange(slots, dtype=jnp.int32)
    panel_of = jnp.sum(
        jnp.where(panel_owner[0][None, :] == slot_ids[:, None], slot_ids[None, :], 0), axis=1
    )
    arrive = arrival_order(place // 2, chips)
    keep_panels, give_panels = panel_of[2 * arrive + core], panel_of[2 * arrive + 1 - core]
    if rows % 128 == 0:
        spread_keep, spread_give = transpose_spread(sep_spread[0], keep_panels, give_panels, rows)
    else:
        panels = sep_spread[0].reshape(2, cells, slots, rows)
        spread_keep, spread_give = (
            jnp.swapaxes(jnp.take(panels, which, axis=2).reshape(2, cells, total // 2), 1, 2)
            for which in (keep_panels, give_panels)
        )
    spread = join(spread_keep, pair(spread_give), 2)

    sep = transpose_sep(sep_inverse[0])

    def solve(level, before=None, subtract=False, **given):
        leaf_values, sums = leaf_and_gather(level, leaf, gather, **given)
        half_sums = sum_chips(sums).astype(BF16)
        other_sums = pair(half_sums)
        own_rows = sep_rows(level, half_sums, sep, False)
        own_rows = sep_rows(level, other_sums, sep, True, own_rows)
        part = spread_cells(level, gather_chips(own_rows), spread)
        return finish(level, leaf_values, part, pair(part), before, subtract)

    def hop(sent, source_layer, target_layer):
        return lax.ppermute(sent, "layer", xor_route("layer", source_layer ^ target_layer))

    value, sent = solve(0, sources=sources)
    for level in range(1, depth):
        arrived = hop(sent, level - 1, level)
        value, sent = solve(level, value, sources=sources, couple=above, arrived=arrived)
    for level in range(depth - 2, -1, -1):
        arrived = hop(sent, level + 1, level)
        value, sent = solve(level, value, True, couple=below, arrived=arrived)
    return value[:, :cells].reshape(1, 2, 4, cells)


def solution(mesh):
    return jax.shard_map(
        local,
        mesh=mesh,
        in_specs=(
            P("layer", None, None, "front"),
            P("layer", None, "front", None),
            P("layer", None, "front", None),
            P("layer", None, "front", None),
            P("layer", None, None, "front"),
            P("layer", None, "front", None),
            P("layer", None, "front", None),
            P("layer", None),
        ),
        out_specs=P("layer", None, None, "front"),
        check_vma=False,
    )
```

```python
import jax
import jax.numpy as jnp
from jax import lax
from jax.experimental import pallas as pl
from jax.experimental.pallas import tpu as pltpu
from jax.sharding import PartitionSpec as P

FEW_CHIPS = 8
BF16, F32 = jnp.bfloat16, jnp.float32
VMEM = pl.BlockSpec(memory_space=pltpu.VMEM)
SMEM = pl.BlockSpec(memory_space=pltpu.SMEM)
ANY = pl.BlockSpec(memory_space=pl.ANY)
MIB = 2**20


def xor_route(axis, distance):
    return [(i, i ^ distance) for i in range(lax.axis_size(axis))]


def pair(block):
    return lax.ppermute(block, "front", xor_route("front", 1))


def same_core_groups():
    slots = lax.axis_size("front")
    return [list(range(core, slots, 2)) for core in range(2)]


def arrival_order(chip, chips):
    steps = jnp.arange(chips, dtype=jnp.int32)
    return chip ^ ((chips - steps) % chips) if chips <= FEW_CHIPS else steps


def from_chips(block, chips):
    return [block] + [
        lax.ppermute(block, "front", xor_route("front", 2 * (chips - step)))
        for step in range(1, chips)
    ]


def gather_chips(block):
    chips = lax.axis_size("front") // 2
    if chips > FEW_CHIPS:
        groups = same_core_groups()
        return lax.all_gather(block, "front", axis=1, tiled=True, axis_index_groups=groups)
    return jnp.concatenate(from_chips(block, chips), axis=1)


def sum_chips(block, after=None):
    chips = lax.axis_size("front") // 2
    if chips > FEW_CHIPS:
        groups = same_core_groups()
        return lax.psum(block.astype(F32), "front", axis_index_groups=groups).astype(BF16)
    parts = from_chips(block, chips)
    if after is None:
        return sum(part.astype(F32) for part in parts).astype(BF16)
    return add_parts(parts, after)


def in_vmem(block):
    return pltpu.with_memory_space_constraint(block, pltpu.VMEM)


def in_hbm(block):
    return pltpu.with_memory_space_constraint(block, pltpu.HBM)


def params(mib):
    return pltpu.CompilerParams(vmem_limit_bytes=mib * MIB)


def cost(flops, nbytes):
    return pl.CostEstimate(flops=flops, bytes_accessed=nbytes, transcendentals=0)


def turned(vector):
    count = vector.shape[0] // 2
    return jnp.concatenate([-vector[count:], vector[:count]], axis=0)


def operands(vector):
    return vector.astype(BF16), turned(vector).astype(BF16)


def times(vector, real_matrix, imag_matrix, contract):
    straight, cross = operands(vector)
    dims = (((1,), (contract,)), ((), ()))
    return lax.dot_general(
        straight, real_matrix, dims, preferred_element_type=F32
    ) + lax.dot_general(cross, imag_matrix, dims, preferred_element_type=F32)


def transpose_sep(sep, after):
    _, rows, total = sep.shape
    step = 128 if rows % 128 == 0 else rows
    chunks = [(part, at) for part in range(2) for at in range(0, rows, step)]

    def kernel(sep_ref, _, out, stored, done):
        copies = []
        for index, (part, at) in enumerate(chunks):
            piece = (part, pl.ds(at, step))
            copy = pltpu.make_async_copy(sep_ref.at[piece], stored.at[piece], done.at[index])
            copy.start()
            copies.append(copy)
        for copy, (part, at) in zip(copies, chunks):
            copy.wait()
            out[part, :, pl.ds(at, step)] = stored[part, pl.ds(at, step), :].T

    return pl.pallas_call(
        kernel,
        in_specs=[ANY, ANY],
        out_specs=VMEM,
        out_shape=pltpu.VMEM((2, total, rows), BF16),
        scratch_shapes=[pltpu.VMEM(sep.shape, BF16), pltpu.SemaphoreType.DMA((len(chunks),))],
        compiler_params=params(18),
        cost_estimate=cost(0, 4 * sep.size),
        name="transpose_sep",
    )(in_hbm(sep), after)


def hold(blocks, after):
    def kernel(*refs):
        del refs

    return pl.pallas_call(
        kernel,
        in_specs=[VMEM] * len(blocks) + [ANY],
        out_specs=[VMEM] * len(blocks),
        out_shape=[pltpu.VMEM(block.shape, block.dtype) for block in blocks],
        input_output_aliases={index: index for index in range(len(blocks))},
        compiler_params=params(1),
        name="hold",
    )(*[in_vmem(block) for block in blocks], after)


def transpose_gather(own, theirs, after):
    _, total, cells = own.shape
    half = total // 2
    step = 512

    def kernel(own_ref, theirs_ref, _, out):
        start = (lax.axis_index("front") % 2) * half
        for side, block in enumerate((own_ref, theirs_ref)):
            for part in range(2):
                for at in range(0, half, step):
                    rows = pl.ds(pl.multiple_of(start + at, step), step)
                    out[part, pl.ds(side * cells, cells), pl.ds(at, step)] = block[part, rows, :].T

    return pl.pallas_call(
        kernel,
        in_specs=[VMEM, VMEM, ANY],
        out_specs=VMEM,
        out_shape=pltpu.VMEM((2, 2 * cells, half), BF16),
        compiler_params=params(16),
        cost_estimate=cost(0, 4 * own.size),
        name="transpose_gather",
    )(in_vmem(own), in_vmem(theirs), after)


def panel_columns(owner_ref, step, rows):
    slots = owner_ref.shape[0]
    place = lax.axis_index("front")
    chips = slots // 2
    chip = place // 2 ^ ((chips - step) % chips) if chips <= FEW_CHIPS else step
    panel = jnp.int32(0)
    for at in range(1, slots):
        panel = jnp.where(owner_ref[at] == 2 * chip + place % 2, at, panel)
    return pl.ds(pl.multiple_of(panel * rows, 128), rows)


def transpose_spread(own, theirs, owner, rows, after):
    _, cells, total = own.shape
    chips = owner.shape[0] // 2

    def kernel(owner_ref, own_ref, theirs_ref, _, out):
        for step in range(chips):
            columns = panel_columns(owner_ref, step, rows)
            for side, block in enumerate((own_ref, theirs_ref)):
                for part in range(2):
                    out[part, pl.ds(step * rows, rows), pl.ds(side * cells, cells)] = block[
                        part, :, columns
                    ].T

    return pl.pallas_call(
        kernel,
        in_specs=[SMEM, VMEM, VMEM, ANY],
        out_specs=VMEM,
        out_shape=pltpu.VMEM((2, total // 2, 2 * cells), BF16),
        compiler_params=params(16),
        cost_estimate=cost(0, 4 * own.size),
        name="transpose_spread",
    )(owner, in_vmem(own), in_vmem(theirs), after)


def take_spread(own, theirs, owner, rows):
    _, cells, total = own.shape
    slots = owner.shape[0]
    place = lax.axis_index("front")
    slot_ids = jnp.arange(slots, dtype=jnp.int32)
    panel_of = jnp.sum(jnp.where(owner[None, :] == slot_ids[:, None], slot_ids[None, :], 0), axis=1)
    wanted = panel_of[2 * arrival_order(place // 2, slots // 2) + place % 2]

    def columns(spread):
        chosen = jnp.take(spread.reshape(2, cells, slots, rows), wanted, axis=2)
        return jnp.swapaxes(chosen.reshape(2, cells, total // 2), 1, 2)

    return jnp.concatenate([columns(own), columns(theirs)], axis=2)


def first_spread_cells(stored, own, theirs, owner, rows):
    _, cells, _ = own.shape
    chips = owner.shape[0] // 2

    def kernel(owner_ref, stored_ref, own_ref, theirs_ref, out):
        @pl.when(lax.axis_index("layer") == 0)
        def _():
            for side, block in enumerate((own_ref, theirs_ref)):
                value = jnp.zeros((8, cells), F32)
                for step in range(chips):
                    columns = panel_columns(owner_ref, step, rows)
                    vector = stored_ref[:, pl.ds(step * rows, rows)].astype(F32)
                    value += times(vector, block[0, :, columns], block[1, :, columns], 1)
                out[:, pl.ds(side * cells, cells)] = value

    return pl.pallas_call(
        kernel,
        in_specs=[SMEM, VMEM, VMEM, VMEM],
        out_specs=VMEM,
        out_shape=jax.ShapeDtypeStruct((8, 2 * cells), F32),
        compiler_params=params(16),
        cost_estimate=cost(16 * own.size, 2 * own.size),
        name="first_spread_cells",
    )(owner, stored, in_vmem(own), in_vmem(theirs))


def add_parts(parts, after):
    def kernel(*refs):
        out = refs[-1]
        total = refs[0][...].astype(F32)
        for part in refs[1 : len(parts)]:
            total = total + part[...].astype(F32)
        out[...] = total.astype(BF16)

    return pl.pallas_call(
        kernel,
        in_specs=[VMEM] * len(parts) + [ANY],
        out_specs=VMEM,
        out_shape=jax.ShapeDtypeStruct(parts[0].shape, BF16),
        compiler_params=params(16),
        cost_estimate=cost(4 * parts[0].size, 10 * parts[0].size),
        name="add_parts",
    )(*parts, in_vmem(after))


def first_leaf_and_gather(sources, leaf, gather, spread):
    cells = leaf.shape[1]
    half = gather.shape[1] // 2

    def kernel(*refs):
        sources_hbm, leaf_hbm, gather_hbm, spread_hbm, leaf_out, keep, give = refs[:7]
        gather_ref, spread_ref, sources_ref, leaf_ref, done = refs[7:]
        core = lax.axis_index("front") % 2
        layer = lax.axis_index("layer")
        sides = [pl.ds(pl.multiple_of(side * half, half), half) for side in (1 - core, core)]
        copies = [
            pltpu.make_async_copy(sources_hbm, sources_ref, done.at[0]),
            pltpu.make_async_copy(leaf_hbm, leaf_ref, done.at[1]),
        ]
        for rows in sides:
            for part in range(2):
                copies.append(
                    pltpu.make_async_copy(
                        gather_hbm.at[part, rows], gather_ref.at[part, rows], done.at[len(copies)]
                    )
                )
        copies.append(pltpu.make_async_copy(spread_hbm, spread_ref, done.at[len(copies)]))
        for copy in copies:
            copy.start()
        copies[0].wait()
        copies[1].wait()

        @pl.when(layer == 0)
        def _():
            source = jnp.concatenate([sources_ref[0], sources_ref[1]], axis=0)
            leaf_out[...] = times(source, leaf_ref[0], leaf_ref[1], 1)

        for index, (out, rows) in enumerate(zip((give, keep), sides)):
            copies[2 + 2 * index].wait()
            copies[3 + 2 * index].wait()

            @pl.when(layer == 0)
            def _(out=out, rows=rows):
                value = times(leaf_out[...], gather_ref[0, rows, :], gather_ref[1, rows, :], 1)
                out[...] = value.astype(out.dtype)

        copies[-1].wait()

    return pl.pallas_call(
        kernel,
        in_specs=[ANY] * 4,
        out_specs=[VMEM] * 5,
        out_shape=[
            jax.ShapeDtypeStruct((8, cells), F32),
            jax.ShapeDtypeStruct((8, half), F32),
            jax.ShapeDtypeStruct((8, half), BF16),
            pltpu.VMEM(gather.shape, BF16),
            pltpu.VMEM(spread.shape, BF16),
        ],
        scratch_shapes=[
            pltpu.VMEM(sources.shape, F32),
            pltpu.VMEM(leaf.shape, BF16),
            pltpu.SemaphoreType.DMA((7,)),
        ],
        compiler_params=params(16),
        cost_estimate=cost(16 * gather.size, 2 * gather.size),
        name="first_leaf_and_gather",
    )(in_hbm(sources), in_hbm(leaf), in_hbm(gather), in_hbm(spread))


def leaf_and_gather(level, leaf, gather, couple, arrived, sources=None):
    cells = leaf[0].shape[1]
    width = gather.shape[2]
    given = [arrived] if sources is None else [arrived, sources]
    mats = list(couple) + list(leaf)

    def kernel(*refs):
        vectors = list(refs[: len(given)])
        matrices = list(refs[len(given) : len(given) + len(mats)])
        gather_ref, leaf_out, sums_out = refs[-3:]

        def blocks(vector, pair_of):
            return jnp.concatenate(
                [
                    times(vector[:, i * cells : (i + 1) * cells], pair_of[i][0], pair_of[i][1], 1)
                    for i in range(2)
                ],
                axis=1,
            )

        @pl.when(lax.axis_index("layer") == level)
        def _():
            source = blocks(vectors[0][...].astype(F32), matrices[:2])
            if sources is not None:
                source = vectors[1][...] - source
            leaf_values = blocks(source, matrices[-2:])
            leaf_out[...] = leaf_values
            sums_out[...] = times(leaf_values, gather_ref[0], gather_ref[1], 0).astype(BF16)

    return pl.pallas_call(
        kernel,
        in_specs=[VMEM] * (len(given) + len(mats) + 1),
        out_specs=[VMEM, VMEM],
        out_shape=[
            jax.ShapeDtypeStruct((8, 2 * cells), F32),
            jax.ShapeDtypeStruct((8, width), BF16),
        ],
        compiler_params=params(16),
        cost_estimate=cost(32 * gather.size, 2 * gather.size),
        name="leaf_and_gather",
    )(*given, *mats, in_vmem(gather))


def sep_rows(level, sums, sep, other, before=None):
    half = sums.shape[1]
    rows = sep.shape[2]
    given = [sums] if before is None else [sums, before]

    def kernel(*refs):
        sums_ref, sep_ref, out = refs[0], refs[-2], refs[-1]

        @pl.when(lax.axis_index("layer") == level)
        def _():
            core = lax.axis_index("front") % 2
            side = 1 - core if other else core
            at = pl.ds(pl.multiple_of(side * half, half), half)
            value = times(sums_ref[...].astype(F32), sep_ref[0, at, :], sep_ref[1, at, :], 0)
            if before is not None:
                value = value + refs[1][...]
            out[...] = value.astype(out.dtype)

    return pl.pallas_call(
        kernel,
        in_specs=[VMEM] * (len(given) + 1),
        out_specs=VMEM,
        out_shape=jax.ShapeDtypeStruct((8, rows), F32 if before is None else BF16),
        compiler_params=params(16),
        cost_estimate=cost(16 * sep.size, sep.size),
        name="sep_rows",
    )(*given, in_vmem(sep))


def spread_cells(level, stored, spread):
    def kernel(stored_ref, spread_ref, out):
        @pl.when(lax.axis_index("layer") == level)
        def _():
            out[...] = times(stored_ref[...].astype(F32), spread_ref[0], spread_ref[1], 0)

    return pl.pallas_call(
        kernel,
        in_specs=[VMEM, VMEM],
        out_specs=VMEM,
        out_shape=jax.ShapeDtypeStruct((8, spread.shape[2]), F32),
        compiler_params=params(16),
        cost_estimate=cost(32 * spread.size, 2 * spread.size),
        name="spread_cells",
    )(stored, in_vmem(spread))


def finish(level, leaf_values, part, theirs, before=None, subtract=False, last=False):
    cells = part.shape[1] // 2
    given = [leaf_values, part, theirs] + ([] if before is None else [before])

    def kernel(*refs):
        leaf_ref, part_ref, theirs_ref = refs[:3]
        here = lax.axis_index("layer") == level

        def store(value):
            if last:
                refs[-1][0, 0] = value[:4, :cells]
                refs[-1][0, 1] = value[4:, :cells]
            else:
                refs[-2][...] = value
                refs[-1][...] = value.astype(BF16)

        @pl.when(here)
        def _():
            swapped = jnp.concatenate([theirs_ref[:, cells:], theirs_ref[:, :cells]], axis=1)
            solved = leaf_ref[...] - (part_ref[...] + swapped)
            if subtract:
                solved = refs[3][...] - solved
            store(solved)

        if before is not None:

            @pl.when(jnp.logical_not(here))
            def _():
                store(refs[3][...])

    if last:
        out_shape = jax.ShapeDtypeStruct((1, 2, 4, cells), F32)
    else:
        out_shape = [jax.ShapeDtypeStruct(part.shape, dtype) for dtype in (F32, BF16)]
    return pl.pallas_call(
        kernel,
        in_specs=[VMEM] * len(given),
        out_specs=VMEM if last else [VMEM, VMEM],
        out_shape=out_shape,
        compiler_params=params(16),
        cost_estimate=cost(4 * part.size, 16 * part.size),
        name="finish",
    )(*given)


def local(
    right_sides,
    leaf_inverse,
    couple_above,
    couple_below,
    sep_gather,
    sep_inverse,
    sep_spread,
    panel_owner,
):
    depth = lax.axis_size("layer")
    cells = leaf_inverse.shape[2]
    rows = sep_inverse.shape[2]
    own_leaf, own_sources = leaf_inverse[0], right_sides[0]

    def with_partner(block):
        return [block, pair(block)]

    own_values, keep_sums, give_sums, own_gather, own_spread = first_leaf_and_gather(
        own_sources, own_leaf, sep_gather[0], sep_spread[0]
    )
    first_sums = (keep_sums + pair(give_sums).astype(F32)).astype(BF16)
    first_values = jnp.concatenate(with_partner(own_values), axis=1)

    leaf = with_partner(own_leaf)
    above = with_partner(couple_above[0])
    below = with_partner(couple_below[0])
    sources = jnp.concatenate(with_partner(own_sources.reshape(8, cells)), axis=1)

    own_gather, own_spread = hold([own_gather, own_spread], first_sums)
    their_gather, their_spread = pair(own_gather), pair(own_spread)
    sep = transpose_sep(sep_inverse[0], first_sums)

    def own_rows_of(level, half_sums):
        other_sums = pair(half_sums)
        own_rows = sep_rows(level, half_sums, sep, False)
        return sep_rows(level, other_sums, sep, True, own_rows)

    def solve(level, before, subtract=False, last=False, **given):
        leaf_values, sums = leaf_and_gather(level, leaf, gather, **given)
        stored = gather_chips(own_rows_of(level, sum_chips(sums)))
        part = spread_cells(level, stored, spread)
        return finish(level, leaf_values, part, pair(part), before, subtract, last)

    def hop(sent, source_layer, target_layer):
        return lax.ppermute(sent, "layer", xor_route("layer", source_layer ^ target_layer))

    stored = gather_chips(own_rows_of(0, sum_chips(first_sums, sep)))
    spreads = own_spread, their_spread, panel_owner[0], rows
    if rows % 128 == 0:
        part = first_spread_cells(stored, *spreads)
    else:
        spread = take_spread(*spreads)
        part = spread_cells(0, stored, spread)
    value, sent = finish(0, first_values, part, pair(part))
    arrived = hop(sent, 0, 1)
    gather = transpose_gather(own_gather, their_gather, sent)
    if rows % 128 == 0:
        spread = transpose_spread(*spreads, sent)

    for level in range(1, depth):
        if level > 1:
            arrived = hop(sent, level - 1, level)
        value, sent = solve(level, value, sources=sources, couple=above, arrived=arrived)
    for level in range(depth - 2, 0, -1):
        arrived = hop(sent, level + 1, level)
        value, sent = solve(level, value, True, couple=below, arrived=arrived)
    return solve(0, value, True, True, couple=below, arrived=hop(sent, 1, 0))


def solution(mesh):
    return jax.shard_map(
        local,
        mesh=mesh,
        in_specs=(
            P("layer", None, None, "front"),
            P("layer", None, "front", None),
            P("layer", None, "front", None),
            P("layer", None, "front", None),
            P("layer", None, None, "front"),
            P("layer", None, "front", None),
            P("layer", None, "front", None),
            P("layer", None),
        ),
        out_specs=P("layer", None, None, "front"),
        check_vma=False,
    )
```

```python
import jax
import jax.numpy as jnp
from jax import lax
from jax.experimental import pallas as pl
from jax.experimental.pallas import tpu as pltpu
from jax.sharding import PartitionSpec as P

FEW_CHIPS = 8
BF16, F32 = jnp.bfloat16, jnp.float32
VMEM = pl.BlockSpec(memory_space=pltpu.VMEM)
SMEM = pl.BlockSpec(memory_space=pltpu.SMEM)
ANY = pl.BlockSpec(memory_space=pl.ANY)
MIB = 2**20


def xor_route(axis, distance):
    return [(i, i ^ distance) for i in range(lax.axis_size(axis))]


def pair(block):
    return lax.ppermute(block, "front", xor_route("front", 1))


def same_core_groups():
    slots = lax.axis_size("front")
    return [list(range(core, slots, 2)) for core in range(2)]


def arrival_order(chip, chips):
    steps = jnp.arange(chips, dtype=jnp.int32)
    return chip ^ ((chips - steps) % chips) if chips <= FEW_CHIPS else steps


def from_chips(block, chips):
    return [block] + [
        lax.ppermute(block, "front", xor_route("front", 2 * (chips - step)))
        for step in range(1, chips)
    ]


def gather_chips(block):
    chips = lax.axis_size("front") // 2
    if chips > FEW_CHIPS:
        groups = same_core_groups()
        return lax.all_gather(block, "front", axis=1, tiled=True, axis_index_groups=groups)
    return jnp.concatenate(from_chips(block, chips), axis=1)


def hop(block, source_layer, target_layer):
    slots = lax.axis_size("front")
    others = [i for i in range(lax.axis_size("layer")) if i not in (source_layer, target_layer)]
    order = [source_layer, target_layer] + others
    target = dict(zip(order, order[1:] + order[:1]))
    return [
        lax.ppermute(
            block,
            ("layer", "front"),
            [(i * slots + j, target[i] * slots + (j ^ cross)) for i in target for j in range(slots)],
        )
        for cross in range(2)
    ]


def sum_chips(block, after=None):
    chips = lax.axis_size("front") // 2
    if chips > FEW_CHIPS:
        groups = same_core_groups()
        return lax.psum(block.astype(F32), "front", axis_index_groups=groups).astype(BF16)
    parts = from_chips(block, chips)
    if after is None:
        return sum(part.astype(F32) for part in parts).astype(BF16)
    return add_parts(parts, after)


def in_vmem(block):
    return pltpu.with_memory_space_constraint(block, pltpu.VMEM)


def in_hbm(block):
    return pltpu.with_memory_space_constraint(block, pltpu.HBM)


def params(mib):
    return pltpu.CompilerParams(vmem_limit_bytes=mib * MIB)


def cost(flops, nbytes):
    return pl.CostEstimate(flops=flops, bytes_accessed=nbytes, transcendentals=0)


def turned(vector):
    count = vector.shape[0] // 2
    return jnp.concatenate([-vector[count:], vector[:count]], axis=0)


def operands(vector):
    return vector.astype(BF16), turned(vector).astype(BF16)


def times(vector, real_matrix, imag_matrix, contract):
    straight, cross = operands(vector)
    dims = (((1,), (contract,)), ((), ()))
    return lax.dot_general(
        straight, real_matrix, dims, preferred_element_type=F32
    ) + lax.dot_general(cross, imag_matrix, dims, preferred_element_type=F32)


def transpose_sep(sep, after):
    _, rows, total = sep.shape
    step = 128 if rows % 128 == 0 else rows
    chunks = [(part, at) for part in range(2) for at in range(0, rows, step)]

    def kernel(sep_ref, _, out, stored, done):
        copies = []
        for index, (part, at) in enumerate(chunks):
            piece = (part, pl.ds(at, step))
            copy = pltpu.make_async_copy(sep_ref.at[piece], stored.at[piece], done.at[index])
            copy.start()
            copies.append(copy)
        for copy, (part, at) in zip(copies, chunks):
            copy.wait()
            out[part, :, pl.ds(at, step)] = stored[part, pl.ds(at, step), :].T

    return pl.pallas_call(
        kernel,
        in_specs=[ANY, ANY],
        out_specs=VMEM,
        out_shape=pltpu.VMEM((2, total, rows), BF16),
        scratch_shapes=[pltpu.VMEM(sep.shape, BF16), pltpu.SemaphoreType.DMA((len(chunks),))],
        compiler_params=params(18),
        cost_estimate=cost(0, 4 * sep.size),
        name="transpose_sep",
    )(in_hbm(sep), after)


def hold(blocks, after):
    def kernel(*refs):
        del refs

    return pl.pallas_call(
        kernel,
        in_specs=[VMEM] * len(blocks) + [ANY],
        out_specs=[VMEM] * len(blocks),
        out_shape=[pltpu.VMEM(block.shape, block.dtype) for block in blocks],
        input_output_aliases={index: index for index in range(len(blocks))},
        compiler_params=params(1),
        name="hold",
    )(*[in_vmem(block) for block in blocks], after)


def transpose_gather(own, theirs, after):
    _, total, cells = own.shape
    half = total // 2
    step = 512

    def kernel(own_ref, theirs_ref, _, out):
        start = (lax.axis_index("front") % 2) * half
        for side, block in enumerate((own_ref, theirs_ref)):
            for part in range(2):
                for at in range(0, half, step):
                    rows = pl.ds(pl.multiple_of(start + at, step), step)
                    out[part, pl.ds(side * cells, cells), pl.ds(at, step)] = block[part, rows, :].T

    return pl.pallas_call(
        kernel,
        in_specs=[VMEM, VMEM, ANY],
        out_specs=VMEM,
        out_shape=pltpu.VMEM((2, 2 * cells, half), BF16),
        compiler_params=params(16),
        cost_estimate=cost(0, 4 * own.size),
        name="transpose_gather",
    )(in_vmem(own), in_vmem(theirs), after)


def panel_columns(owner_ref, step, rows):
    slots = owner_ref.shape[0]
    place = lax.axis_index("front")
    chips = slots // 2
    chip = place // 2 ^ ((chips - step) % chips) if chips <= FEW_CHIPS else step
    panel = jnp.int32(0)
    for at in range(1, slots):
        panel = jnp.where(owner_ref[at] == 2 * chip + place % 2, at, panel)
    return pl.ds(pl.multiple_of(panel * rows, 128), rows)


def transpose_spread(own, theirs, owner, rows, after):
    _, cells, total = own.shape
    chips = owner.shape[0] // 2

    def kernel(owner_ref, own_ref, theirs_ref, _, out):
        for step in range(chips):
            columns = panel_columns(owner_ref, step, rows)
            for side, block in enumerate((own_ref, theirs_ref)):
                for part in range(2):
                    out[part, pl.ds(step * rows, rows), pl.ds(side * cells, cells)] = block[
                        part, :, columns
                    ].T

    return pl.pallas_call(
        kernel,
        in_specs=[SMEM, VMEM, VMEM, ANY],
        out_specs=VMEM,
        out_shape=pltpu.VMEM((2, total // 2, 2 * cells), BF16),
        compiler_params=params(16),
        cost_estimate=cost(0, 4 * own.size),
        name="transpose_spread",
    )(owner, in_vmem(own), in_vmem(theirs), after)


def take_spread(own, theirs, owner, rows):
    _, cells, total = own.shape
    slots = owner.shape[0]
    place = lax.axis_index("front")
    slot_ids = jnp.arange(slots, dtype=jnp.int32)
    panel_of = jnp.sum(jnp.where(owner[None, :] == slot_ids[:, None], slot_ids[None, :], 0), axis=1)
    wanted = panel_of[2 * arrival_order(place // 2, slots // 2) + place % 2]

    def columns(spread):
        chosen = jnp.take(spread.reshape(2, cells, slots, rows), wanted, axis=2)
        return jnp.swapaxes(chosen.reshape(2, cells, total // 2), 1, 2)

    return jnp.concatenate([columns(own), columns(theirs)], axis=2)


def first_spread_cells(stored, leaf_values, own, theirs, owner, rows):
    _, cells, _ = own.shape
    chips = owner.shape[0] // 2

    def kernel(owner_ref, stored_ref, leaf_ref, own_ref, theirs_ref, part_out, share_out):
        @pl.when(lax.axis_index("layer") == 0)
        def _():
            for side, block in enumerate((own_ref, theirs_ref)):
                value = jnp.zeros((8, cells), F32)
                for step in range(chips):
                    columns = panel_columns(owner_ref, step, rows)
                    vector = stored_ref[:, pl.ds(step * rows, rows)].astype(F32)
                    value += times(vector, block[0, :, columns], block[1, :, columns], 1)
                part_out[:, pl.ds(side * cells, cells)] = value
            share_out[...] = share_of_value(part_out[...], leaf_ref[...], None, False)

    return pl.pallas_call(
        kernel,
        in_specs=[SMEM] + [VMEM] * 4,
        out_specs=[VMEM, VMEM],
        out_shape=[jax.ShapeDtypeStruct((8, 2 * cells), F32)] * 2,
        compiler_params=params(16),
        cost_estimate=cost(16 * own.size, 2 * own.size),
        name="first_spread_cells",
    )(owner, stored, leaf_values, in_vmem(own), in_vmem(theirs))


def add_parts(parts, after):
    def kernel(*refs):
        out = refs[-1]
        total = refs[0][...].astype(F32)
        for part in refs[1 : len(parts)]:
            total = total + part[...].astype(F32)
        out[...] = total.astype(BF16)

    return pl.pallas_call(
        kernel,
        in_specs=[VMEM] * len(parts) + [ANY],
        out_specs=VMEM,
        out_shape=jax.ShapeDtypeStruct(parts[0].shape, BF16),
        compiler_params=params(16),
        cost_estimate=cost(4 * parts[0].size, 10 * parts[0].size),
        name="add_parts",
    )(*parts, in_vmem(after))


def first_leaf_and_gather(sources, leaf, gather, spread):
    cells = leaf.shape[1]
    half = gather.shape[1] // 2

    def kernel(*refs):
        sources_hbm, leaf_hbm, gather_hbm, spread_hbm, leaf_out, keep, give = refs[:7]
        gather_ref, spread_ref, sources_ref, leaf_ref, done = refs[7:]
        core = lax.axis_index("front") % 2
        layer = lax.axis_index("layer")
        sides = [pl.ds(pl.multiple_of(side * half, half), half) for side in (1 - core, core)]
        copies = [
            pltpu.make_async_copy(sources_hbm, sources_ref, done.at[0]),
            pltpu.make_async_copy(leaf_hbm, leaf_ref, done.at[1]),
        ]
        for rows in sides:
            for part in range(2):
                copies.append(
                    pltpu.make_async_copy(
                        gather_hbm.at[part, rows], gather_ref.at[part, rows], done.at[len(copies)]
                    )
                )
        copies.append(pltpu.make_async_copy(spread_hbm, spread_ref, done.at[len(copies)]))
        for copy in copies:
            copy.start()
        copies[0].wait()
        copies[1].wait()

        @pl.when(layer == 0)
        def _():
            source = jnp.concatenate([sources_ref[0], sources_ref[1]], axis=0)
            leaf_out[...] = times(source, leaf_ref[0], leaf_ref[1], 1)

        for index, (out, rows) in enumerate(zip((give, keep), sides)):
            copies[2 + 2 * index].wait()
            copies[3 + 2 * index].wait()

            @pl.when(layer == 0)
            def _(out=out, rows=rows):
                value = times(leaf_out[...], gather_ref[0, rows, :], gather_ref[1, rows, :], 1)
                out[...] = value.astype(out.dtype)

        copies[-1].wait()

    return pl.pallas_call(
        kernel,
        in_specs=[ANY] * 4,
        out_specs=[VMEM] * 5,
        out_shape=[
            jax.ShapeDtypeStruct((8, cells), F32),
            jax.ShapeDtypeStruct((8, half), F32),
            jax.ShapeDtypeStruct((8, half), BF16),
            pltpu.VMEM(gather.shape, BF16),
            pltpu.VMEM(spread.shape, BF16),
        ],
        scratch_shapes=[
            pltpu.VMEM(sources.shape, F32),
            pltpu.VMEM(leaf.shape, BF16),
            pltpu.SemaphoreType.DMA((7,)),
        ],
        compiler_params=params(16),
        cost_estimate=cost(16 * gather.size, 2 * gather.size),
        name="first_leaf_and_gather",
    )(in_hbm(sources), in_hbm(leaf), in_hbm(gather), in_hbm(spread))


def leaf_and_gather(level, leaf, gather, couple, arrived, sources=None):
    cells = leaf[0].shape[1]
    width = gather.shape[2]
    given = list(arrived) if sources is None else [*arrived, sources]
    mats = list(couple) + list(leaf)

    def kernel(*refs):
        vectors = list(refs[: len(given)])
        matrices = list(refs[len(given) : len(given) + len(mats)])
        gather_ref, leaf_out, sums_out = refs[-3:]

        def blocks(vector, pair_of):
            return jnp.concatenate(
                [
                    times(vector[:, i * cells : (i + 1) * cells], pair_of[i][0], pair_of[i][1], 1)
                    for i in range(2)
                ],
                axis=1,
            )

        @pl.when(lax.axis_index("layer") == level)
        def _():
            crossed = jnp.concatenate([vectors[1][:, cells:], vectors[1][:, :cells]], axis=1)
            source = blocks(vectors[0][...] + crossed, matrices[:2])
            if sources is not None:
                source = vectors[2][...] - source
            leaf_values = blocks(source, matrices[-2:])
            leaf_out[...] = leaf_values
            sums_out[...] = times(leaf_values, gather_ref[0], gather_ref[1], 0).astype(BF16)

    return pl.pallas_call(
        kernel,
        in_specs=[VMEM] * (len(given) + len(mats) + 1),
        out_specs=[VMEM, VMEM],
        out_shape=[
            jax.ShapeDtypeStruct((8, 2 * cells), F32),
            jax.ShapeDtypeStruct((8, width), BF16),
        ],
        compiler_params=params(16),
        cost_estimate=cost(32 * gather.size, 2 * gather.size),
        name="leaf_and_gather",
    )(*given, *mats, in_vmem(gather))


def sep_rows(level, sums, sep, other, before=None):
    half = sums.shape[1]
    rows = sep.shape[2]
    given = [sums] if before is None else [sums, before]

    def kernel(*refs):
        sums_ref, sep_ref, out = refs[0], refs[-2], refs[-1]

        @pl.when(lax.axis_index("layer") == level)
        def _():
            core = lax.axis_index("front") % 2
            side = 1 - core if other else core
            at = pl.ds(pl.multiple_of(side * half, half), half)
            value = times(sums_ref[...].astype(F32), sep_ref[0, at, :], sep_ref[1, at, :], 0)
            if before is not None:
                value = value + refs[1][...]
            out[...] = value.astype(out.dtype)

    return pl.pallas_call(
        kernel,
        in_specs=[VMEM] * (len(given) + 1),
        out_specs=VMEM,
        out_shape=jax.ShapeDtypeStruct((8, rows), F32 if before is None else BF16),
        compiler_params=params(16),
        cost_estimate=cost(16 * sep.size, sep.size),
        name="sep_rows",
    )(*given, in_vmem(sep))


def share_of_value(part, leaf_values, before, subtract):
    first = jnp.where(lax.axis_index("front") % 2 == 0, 1.0, 0.0)
    if subtract:
        return first * (before - leaf_values) + part
    return first * leaf_values - part


def spread_cells(level, stored, spread, leaf_values, before=None, subtract=False):
    given = [stored, leaf_values] + ([before] if subtract else [])

    def kernel(*refs):
        stored_ref, leaf_ref = refs[:2]
        spread_ref, part_out, share_out = refs[-3:]

        @pl.when(lax.axis_index("layer") == level)
        def _():
            part = times(stored_ref[...].astype(F32), spread_ref[0], spread_ref[1], 0)
            part_out[...] = part
            held = refs[2][...] if subtract else None
            share_out[...] = share_of_value(part, leaf_ref[...], held, subtract)

    return pl.pallas_call(
        kernel,
        in_specs=[VMEM] * (len(given) + 1),
        out_specs=[VMEM, VMEM],
        out_shape=[jax.ShapeDtypeStruct((8, spread.shape[2]), F32)] * 2,
        compiler_params=params(16),
        cost_estimate=cost(32 * spread.size, 2 * spread.size),
        name="spread_cells",
    )(*given, in_vmem(spread))


def finish(level, leaf_values, part, theirs, before=None, subtract=False, last=False):
    cells = part.shape[1] // 2
    given = [leaf_values, part, theirs] + ([] if before is None else [before])

    def kernel(*refs):
        leaf_ref, part_ref, theirs_ref = refs[:3]
        here = lax.axis_index("layer") == level

        def store(value):
            if last:
                refs[-1][0, 0] = value[:4, :cells]
                refs[-1][0, 1] = value[4:, :cells]
            else:
                refs[-1][...] = value

        @pl.when(here)
        def _():
            swapped = jnp.concatenate([theirs_ref[:, cells:], theirs_ref[:, :cells]], axis=1)
            solved = leaf_ref[...] - (part_ref[...] + swapped)
            if subtract:
                solved = refs[3][...] - solved
            store(solved)

        if before is not None:

            @pl.when(jnp.logical_not(here))
            def _():
                store(refs[3][...])

    return pl.pallas_call(
        kernel,
        in_specs=[VMEM] * len(given),
        out_specs=VMEM,
        out_shape=jax.ShapeDtypeStruct((1, 2, 4, cells) if last else part.shape, F32),
        compiler_params=params(16),
        cost_estimate=cost(4 * part.size, 16 * part.size),
        name="finish",
    )(*given)


def local(
    right_sides,
    leaf_inverse,
    couple_above,
    couple_below,
    sep_gather,
    sep_inverse,
    sep_spread,
    panel_owner,
):
    depth = lax.axis_size("layer")
    cells = leaf_inverse.shape[2]
    rows = sep_inverse.shape[2]
    own_leaf, own_sources = leaf_inverse[0], right_sides[0]

    def with_partner(block):
        return [block, pair(block)]

    own_values, keep_sums, give_sums, own_gather, own_spread = first_leaf_and_gather(
        own_sources, own_leaf, sep_gather[0], sep_spread[0]
    )
    first_sums = (keep_sums + pair(give_sums).astype(F32)).astype(BF16)
    first_values = jnp.concatenate(with_partner(own_values), axis=1)

    leaf = with_partner(own_leaf)
    above = with_partner(couple_above[0])
    below = with_partner(couple_below[0])
    sources = jnp.concatenate(with_partner(own_sources.reshape(8, cells)), axis=1)

    own_gather, own_spread = hold([own_gather, own_spread], first_sums)
    their_gather, their_spread = pair(own_gather), pair(own_spread)
    sep = transpose_sep(sep_inverse[0], first_sums)

    def own_rows_of(level, half_sums):
        other_sums = pair(half_sums)
        own_rows = sep_rows(level, half_sums, sep, False)
        return sep_rows(level, other_sums, sep, True, own_rows)

    def solve(level, before, subtract=False, last=False, **given):
        leaf_values, sums = leaf_and_gather(level, leaf, gather, **given)
        stored = gather_chips(own_rows_of(level, sum_chips(sums)))
        part, share = spread_cells(level, stored, spread, leaf_values, before, subtract)
        return finish(level, leaf_values, part, pair(part), before, subtract, last), share

    stored = gather_chips(own_rows_of(0, sum_chips(first_sums, sep)))
    spreads = own_spread, their_spread, panel_owner[0], rows
    if rows % 128 == 0:
        part, share = first_spread_cells(stored, first_values, *spreads)
    else:
        spread = take_spread(*spreads)
        part, share = spread_cells(0, stored, spread, first_values)
    arrived = hop(share, 0, 1)
    value = finish(0, first_values, part, pair(part))
    gather = transpose_gather(own_gather, their_gather, share)
    if rows % 128 == 0:
        spread = transpose_spread(*spreads, share)

    for level in range(1, depth):
        if level > 1:
            arrived = hop(share, level - 1, level)
        value, share = solve(level, value, sources=sources, couple=above, arrived=arrived)
    for level in range(depth - 2, -1, -1):
        arrived = hop(share, level + 1, level)
        value, share = solve(level, value, True, level == 0, couple=below, arrived=arrived)
    return value


def solution(mesh):
    return jax.shard_map(
        local,
        mesh=mesh,
        in_specs=(
            P("layer", None, None, "front"),
            P("layer", None, "front", None),
            P("layer", None, "front", None),
            P("layer", None, "front", None),
            P("layer", None, None, "front"),
            P("layer", None, "front", None),
            P("layer", None, "front", None),
            P("layer", None),
        ),
        out_specs=P("layer", None, None, "front"),
        check_vma=False,
    )
```

```python
import jax
import jax.numpy as jnp
from jax import lax
from jax.experimental import pallas as pl
from jax.experimental.pallas import tpu as pltpu
from jax.sharding import PartitionSpec as P

FEW_CHIPS = 8
BF16, F32 = jnp.bfloat16, jnp.float32
VMEM = pl.BlockSpec(memory_space=pltpu.VMEM)
SMEM = pl.BlockSpec(memory_space=pltpu.SMEM)
ANY = pl.BlockSpec(memory_space=pl.ANY)
MIB = 2**20


def xor_route(axis, distance):
    return [(i, i ^ distance) for i in range(lax.axis_size(axis))]


def pair(block):
    return lax.ppermute(block, "front", xor_route("front", 1))


def same_core_groups():
    slots = lax.axis_size("front")
    return [list(range(core, slots, 2)) for core in range(2)]


def arrival_order(chip, chips):
    steps = jnp.arange(chips, dtype=jnp.int32)
    return chip ^ ((chips - steps) % chips) if chips <= FEW_CHIPS else steps


def from_chips(block, chips):
    return [block] + [
        lax.ppermute(block, "front", xor_route("front", 2 * (chips - step)))
        for step in range(1, chips)
    ]


def gather_chips(block, after=None):
    chips = lax.axis_size("front") // 2
    if chips > FEW_CHIPS:
        groups = same_core_groups()
        return lax.all_gather(block, "front", axis=1, tiled=True, axis_index_groups=groups)
    parts = from_chips(block, chips)
    if after is None:
        return jnp.concatenate(parts, axis=1)
    return join_parts(parts, after)


def hop(block, source_layer, target_layer):
    slots = lax.axis_size("front")
    others = [i for i in range(lax.axis_size("layer")) if i not in (source_layer, target_layer)]
    order = [source_layer, target_layer] + others
    target = dict(zip(order, order[1:] + order[:1]))
    return [
        lax.ppermute(
            block,
            ("layer", "front"),
            [(i * slots + j, target[i] * slots + (j ^ cross)) for i in target for j in range(slots)],
        )
        for cross in range(2)
    ]


def sum_chips(block, after=None):
    chips = lax.axis_size("front") // 2
    if chips > FEW_CHIPS:
        groups = same_core_groups()
        return lax.psum(block.astype(F32), "front", axis_index_groups=groups).astype(BF16)
    parts = from_chips(block, chips)
    if after is None:
        return sum(part.astype(F32) for part in parts).astype(BF16)
    return add_parts(parts, after)


def in_vmem(block):
    return pltpu.with_memory_space_constraint(block, pltpu.VMEM)


def in_hbm(block):
    return pltpu.with_memory_space_constraint(block, pltpu.HBM)


def params(mib):
    return pltpu.CompilerParams(vmem_limit_bytes=mib * MIB)


def cost(flops, nbytes):
    return pl.CostEstimate(flops=flops, bytes_accessed=nbytes, transcendentals=0)


def turned(vector):
    count = vector.shape[0] // 2
    return jnp.concatenate([-vector[count:], vector[:count]], axis=0)


def operands(vector):
    return vector.astype(BF16), turned(vector).astype(BF16)


def times(vector, real_matrix, imag_matrix, contract):
    straight, cross = operands(vector)
    dims = (((1,), (contract,)), ((), ()))
    return lax.dot_general(
        straight, real_matrix, dims, preferred_element_type=F32
    ) + lax.dot_general(cross, imag_matrix, dims, preferred_element_type=F32)


def transpose_sep(sep, after):
    _, rows, total = sep.shape
    step = 128 if rows % 128 == 0 else rows
    chunks = [(part, at) for part in range(2) for at in range(0, rows, step)]

    def kernel(sep_ref, _, out, stored, done):
        copies = []
        for index, (part, at) in enumerate(chunks):
            piece = (part, pl.ds(at, step))
            copy = pltpu.make_async_copy(sep_ref.at[piece], stored.at[piece], done.at[index])
            copy.start()
            copies.append(copy)
        for copy, (part, at) in zip(copies, chunks):
            copy.wait()
            out[part, :, pl.ds(at, step)] = stored[part, pl.ds(at, step), :].T

    return pl.pallas_call(
        kernel,
        in_specs=[ANY, ANY],
        out_specs=VMEM,
        out_shape=pltpu.VMEM((2, total, rows), BF16),
        scratch_shapes=[pltpu.VMEM(sep.shape, BF16), pltpu.SemaphoreType.DMA((len(chunks),))],
        compiler_params=params(18),
        cost_estimate=cost(0, 4 * sep.size),
        name="transpose_sep",
    )(in_hbm(sep), after)


def hold(blocks, after):
    def kernel(*refs):
        del refs

    return pl.pallas_call(
        kernel,
        in_specs=[ANY] * (len(blocks) + 1),
        out_specs=[ANY] * len(blocks),
        out_shape=[jax.ShapeDtypeStruct(block.shape, block.dtype) for block in blocks],
        input_output_aliases={index: index for index in range(len(blocks))},
        compiler_params=params(1),
        name="hold",
    )(*blocks, after)


def transpose_gather(own, theirs, after):
    _, total, cells = own.shape
    half = total // 2
    step = 512

    def kernel(own_ref, theirs_ref, _, out):
        start = (lax.axis_index("front") % 2) * half
        for side, block in enumerate((own_ref, theirs_ref)):
            for part in range(2):
                for at in range(0, half, step):
                    rows = pl.ds(pl.multiple_of(start + at, step), step)
                    out[part, pl.ds(side * cells, cells), pl.ds(at, step)] = block[part, rows, :].T

    return pl.pallas_call(
        kernel,
        in_specs=[VMEM, VMEM, ANY],
        out_specs=VMEM,
        out_shape=pltpu.VMEM((2, 2 * cells, half), BF16),
        compiler_params=params(16),
        cost_estimate=cost(0, 4 * own.size),
        name="transpose_gather",
    )(in_vmem(own), in_vmem(theirs), after)


def panel_columns(owner_ref, step, rows):
    slots = owner_ref.shape[0]
    place = lax.axis_index("front")
    chips = slots // 2
    chip = place // 2 ^ ((chips - step) % chips) if chips <= FEW_CHIPS else step
    panel = jnp.int32(0)
    for at in range(1, slots):
        panel = jnp.where(owner_ref[at] == 2 * chip + place % 2, at, panel)
    return pl.ds(pl.multiple_of(panel * rows, 128), rows)


def transpose_maps(own, theirs, owner, rows, after):
    _, cells, width = own.shape
    slots = owner.shape[0]
    chips = slots // 2

    def kernel(owner_ref, own_ref, theirs_ref, _, out, blocks_out):
        for step in range(chips):
            columns = panel_columns(owner_ref, step, rows)
            for side, block in enumerate((own_ref, theirs_ref)):
                for part in range(2):
                    out[part, pl.ds(step * rows, rows), pl.ds(side * cells, cells)] = block[
                        part, :, columns
                    ].T
        for side, block in enumerate((own_ref, theirs_ref)):
            for kind in range(3):
                columns = pl.ds(slots * rows + kind * cells, cells)
                for part in range(2):
                    blocks_out[side, kind, part] = block[part, :, columns]

    return pl.pallas_call(
        kernel,
        in_specs=[SMEM, VMEM, VMEM, ANY],
        out_specs=[VMEM, VMEM],
        out_shape=[
            pltpu.VMEM((2, chips * rows, 2 * cells), BF16),
            jax.ShapeDtypeStruct((2, 3, 2, cells, cells), BF16),
        ],
        compiler_params=params(16),
        cost_estimate=cost(0, 4 * own.size),
        name="transpose_maps",
    )(owner, in_vmem(own), in_vmem(theirs), after)


def take_maps(own, theirs, owner, rows):
    _, cells, width = own.shape
    slots = owner.shape[0]
    total = slots * rows
    place = lax.axis_index("front")
    slot_ids = jnp.arange(slots, dtype=jnp.int32)
    panel_of = jnp.sum(jnp.where(owner[None, :] == slot_ids[:, None], slot_ids[None, :], 0), axis=1)
    wanted = panel_of[2 * arrival_order(place // 2, slots // 2) + place % 2]

    def columns(maps):
        chosen = jnp.take(maps[:, :, :total].reshape(2, cells, slots, rows), wanted, axis=2)
        return jnp.swapaxes(chosen.reshape(2, cells, total // 2), 1, 2)

    def blocks(maps):
        return jnp.moveaxis(maps[:, :, total:].reshape(2, cells, 3, cells), 2, 0)

    spread = jnp.concatenate([columns(own), columns(theirs)], axis=2)
    return spread, jnp.stack([blocks(own), blocks(theirs)])


def add_parts(parts, after):
    def kernel(*refs):
        out = refs[-1]
        total = refs[0][...].astype(F32)
        for part in refs[1 : len(parts)]:
            total = total + part[...].astype(F32)
        out[...] = total.astype(BF16)

    return pl.pallas_call(
        kernel,
        in_specs=[VMEM] * len(parts) + [ANY],
        out_specs=VMEM,
        out_shape=jax.ShapeDtypeStruct(parts[0].shape, BF16),
        compiler_params=params(16),
        cost_estimate=cost(4 * parts[0].size, 10 * parts[0].size),
        name="add_parts",
    )(*parts, in_vmem(after))


def join_parts(parts, after):
    width = parts[0].shape[1]

    def kernel(*refs):
        out = refs[-1]
        for index, part in enumerate(refs[: len(parts)]):
            out[:, pl.ds(index * width, width)] = part[...]

    return pl.pallas_call(
        kernel,
        in_specs=[VMEM] * len(parts) + [ANY],
        out_specs=VMEM,
        out_shape=jax.ShapeDtypeStruct((8, len(parts) * width), BF16),
        compiler_params=params(16),
        cost_estimate=cost(0, 8 * parts[0].size),
        name="join_parts",
    )(*parts, in_vmem(after))


def first_leaf_and_gather(sources, gather, maps):
    cells = gather.shape[2]
    half = gather.shape[1] // 2
    starts = [sum(block.shape[2] for block in maps[:index]) for index in range(len(maps))]
    width = sum(block.shape[2] for block in maps)

    def kernel(*refs):
        sources_hbm, gather_hbm, *maps_hbm = refs[: 2 + len(maps)]
        keep, give, gather_ref, maps_ref, sources_ref, done = refs[2 + len(maps) :]
        core = lax.axis_index("front") % 2
        layer = lax.axis_index("layer")
        sides = [pl.ds(pl.multiple_of(side * half, half), half) for side in (1 - core, core)]
        leaf_at = pl.ds(starts[1], cells)
        values_at, sources_at = pl.ds(half, cells), pl.ds(half + cells, cells)
        pieces = [(sources_hbm, sources_ref), (maps_hbm[1], maps_ref.at[:, :, leaf_at])]
        for rows in sides:
            for part in range(2):
                pieces.append((gather_hbm.at[part, rows], gather_ref.at[part, rows]))
        for index in (0, 2, 3):
            columns = pl.ds(starts[index], maps[index].shape[2])
            pieces.append((maps_hbm[index], maps_ref.at[:, :, columns]))
        copies = [
            pltpu.make_async_copy(source, target, done.at[index])
            for index, (source, target) in enumerate(pieces)
        ]
        for copy in copies:
            copy.start()
        copies[0].wait()
        copies[1].wait()
        source = jnp.concatenate([sources_ref[0], sources_ref[1]], axis=0)
        for out in (give, keep):
            out[:, sources_at] = source

        @pl.when(layer == 0)
        def _():
            leaf_values = times(source, maps_ref[0, :, leaf_at], maps_ref[1, :, leaf_at], 1)
            for out in (give, keep):
                out[:, values_at] = leaf_values

        for index, (out, rows) in enumerate(zip((give, keep), sides)):
            copies[2 + 2 * index].wait()
            copies[3 + 2 * index].wait()

            @pl.when(layer == 0)
            def _(out=out, rows=rows):
                leaf_values = out[:, values_at]
                out[:, pl.ds(0, half)] = times(
                    leaf_values, gather_ref[0, rows, :], gather_ref[1, rows, :], 1
                )

        for copy in copies[6:]:
            copy.wait()

    return pl.pallas_call(
        kernel,
        in_specs=[ANY] * (2 + len(maps)),
        out_specs=[VMEM] * 4,
        out_shape=[
            jax.ShapeDtypeStruct((8, half + 2 * cells), F32),
            jax.ShapeDtypeStruct((8, half + 2 * cells), F32),
            pltpu.VMEM(gather.shape, BF16),
            pltpu.VMEM((2, cells, width), BF16),
        ],
        scratch_shapes=[pltpu.VMEM(sources.shape, F32), pltpu.SemaphoreType.DMA((9,))],
        compiler_params=params(16),
        cost_estimate=cost(16 * gather.size, 2 * gather.size),
        name="first_leaf_and_gather",
    )(in_hbm(sources), in_hbm(gather), *[in_hbm(block) for block in maps])


def leaf_and_gather(level, blocks, gather, arrived, sources=None):
    cells = blocks.shape[3]
    width = gather.shape[2]
    given = list(arrived) if sources is None else [*arrived, sources]

    def kernel(*refs):
        blocks_ref, gather_ref, leaf_out, sums_out = refs[-4:]

        def apply(vector, kind):
            return jnp.concatenate(
                [
                    times(
                        vector[:, side * cells : (side + 1) * cells],
                        blocks_ref[side, kind, 0],
                        blocks_ref[side, kind, 1],
                        1,
                    )
                    for side in range(2)
                ],
                axis=1,
            )

        @pl.when(lax.axis_index("layer") == level)
        def _():
            crossed = jnp.concatenate([refs[1][:, cells:], refs[1][:, :cells]], axis=1)
            source = apply(refs[0][...] + crossed, 2 if sources is None else 1)
            if sources is not None:
                source = refs[2][...] - source
            leaf_values = apply(source, 0)
            leaf_out[...] = leaf_values
            sums_out[...] = times(leaf_values, gather_ref[0], gather_ref[1], 0).astype(BF16)

    return pl.pallas_call(
        kernel,
        in_specs=[VMEM] * (len(given) + 2),
        out_specs=[VMEM, VMEM],
        out_shape=[
            jax.ShapeDtypeStruct((8, 2 * cells), F32),
            jax.ShapeDtypeStruct((8, width), BF16),
        ],
        compiler_params=params(16),
        cost_estimate=cost(32 * gather.size, 2 * gather.size),
        name="leaf_and_gather",
    )(*given, blocks, in_vmem(gather))


def sep_rows(level, sums, sep, other, before=None):
    half = sums.shape[1]
    rows = sep.shape[2]
    given = [sums] if before is None else [sums, before]

    def kernel(*refs):
        sums_ref, sep_ref, out = refs[0], refs[-2], refs[-1]

        @pl.when(lax.axis_index("layer") == level)
        def _():
            core = lax.axis_index("front") % 2
            side = 1 - core if other else core
            at = pl.ds(pl.multiple_of(side * half, half), half)
            value = times(sums_ref[...].astype(F32), sep_ref[0, at, :], sep_ref[1, at, :], 0)
            if before is not None:
                value = value + refs[1][...]
            out[...] = value.astype(out.dtype)

    return pl.pallas_call(
        kernel,
        in_specs=[VMEM] * (len(given) + 1),
        out_specs=VMEM,
        out_shape=jax.ShapeDtypeStruct((8, rows), F32 if before is None else BF16),
        compiler_params=params(16),
        cost_estimate=cost(16 * sep.size, sep.size),
        name="sep_rows",
    )(*given, in_vmem(sep))


def share_of_value(part, leaf_values, before, subtract):
    first = jnp.where(lax.axis_index("front") % 2 == 0, 1.0, 0.0)
    if subtract:
        return first * (before - leaf_values) + part
    return first * leaf_values - part


def spread_cells(level, stored, spread, leaf_values, before=None, subtract=False):
    given = [stored, leaf_values] + ([before] if subtract else [])

    def kernel(*refs):
        stored_ref, leaf_ref = refs[:2]
        spread_ref, part_out, share_out = refs[-3:]

        @pl.when(lax.axis_index("layer") == level)
        def _():
            part = times(stored_ref[...].astype(F32), spread_ref[0], spread_ref[1], 0)
            part_out[...] = part
            held = refs[2][...] if subtract else None
            share_out[...] = share_of_value(part, leaf_ref[...], held, subtract)

    return pl.pallas_call(
        kernel,
        in_specs=[VMEM] * (len(given) + 1),
        out_specs=[VMEM, VMEM],
        out_shape=[jax.ShapeDtypeStruct((8, spread.shape[2]), F32)] * 2,
        compiler_params=params(16),
        cost_estimate=cost(32 * spread.size, 2 * spread.size),
        name="spread_cells",
    )(*given, in_vmem(spread))


def finish(level, leaf_values, part, theirs, before=None, subtract=False, last=False):
    cells = part.shape[1] // 2
    given = [leaf_values, part, theirs] + ([] if before is None else [before])

    def kernel(*refs):
        leaf_ref, part_ref, theirs_ref = refs[:3]
        here = lax.axis_index("layer") == level

        def store(value):
            if last:
                refs[-1][0, 0] = value[:4, :cells]
                refs[-1][0, 1] = value[4:, :cells]
            else:
                refs[-1][...] = value

        @pl.when(here)
        def _():
            swapped = jnp.concatenate([theirs_ref[:, cells:], theirs_ref[:, :cells]], axis=1)
            solved = leaf_ref[...] - (part_ref[...] + swapped)
            if subtract:
                solved = refs[3][...] - solved
            store(solved)

        if before is not None:

            @pl.when(jnp.logical_not(here))
            def _():
                store(refs[3][...])

    return pl.pallas_call(
        kernel,
        in_specs=[VMEM] * len(given),
        out_specs=VMEM,
        out_shape=jax.ShapeDtypeStruct((1, 2, 4, cells) if last else part.shape, F32),
        compiler_params=params(16),
        cost_estimate=cost(4 * part.size, 16 * part.size),
        name="finish",
    )(*given)


def local(
    right_sides,
    leaf_inverse,
    couple_above,
    couple_below,
    sep_gather,
    sep_inverse,
    sep_spread,
    panel_owner,
):
    depth = lax.axis_size("layer")
    cells = leaf_inverse.shape[2]
    rows = sep_inverse.shape[2]

    maps = [sep_spread[0], leaf_inverse[0], couple_above[0], couple_below[0]]
    keep, give, own_gather, own_maps = first_leaf_and_gather(right_sides[0], sep_gather[0], maps)
    got = pair(give)
    half = sep_gather.shape[2] // 2
    first_sums = (keep[:, :half] + got[:, :half]).astype(BF16)
    first_values, sources = (
        jnp.concatenate([block[:, at : at + cells] for block in (keep, got)], axis=1)
        for at in (half, half + cells)
    )

    own_gather, own_maps = hold([own_gather, own_maps], first_sums)
    their_gather, their_maps = pair(own_gather), pair(own_maps)
    sep = transpose_sep(sep_inverse[0], first_sums)

    def own_rows_of(level, half_sums):
        other_sums = pair(half_sums)
        own_rows = sep_rows(level, half_sums, sep, False)
        return sep_rows(level, other_sums, sep, True, own_rows)

    def solve(level, before, subtract=False, last=False, **given):
        leaf_values, sums = leaf_and_gather(level, blocks, gather, **given)
        stored = gather_chips(own_rows_of(level, sum_chips(sums)))
        part, share = spread_cells(level, stored, spread, leaf_values, before, subtract)
        return finish(level, leaf_values, part, pair(part), before, subtract, last), share

    own_rows = own_rows_of(0, sum_chips(first_sums, sep))
    if rows % 128 == 0:
        spread, blocks = transpose_maps(own_maps, their_maps, panel_owner[0], rows, own_rows)
    else:
        spread, blocks = take_maps(own_maps, their_maps, panel_owner[0], rows)
    part, share = spread_cells(0, gather_chips(own_rows, spread), spread, first_values)
    arrived = hop(share, 0, 1)
    value = finish(0, first_values, part, pair(part))
    gather = transpose_gather(own_gather, their_gather, share)

    for level in range(1, depth):
        if level > 1:
            arrived = hop(share, level - 1, level)
        value, share = solve(level, value, sources=sources, arrived=arrived)
    for level in range(depth - 2, -1, -1):
        arrived = hop(share, level + 1, level)
        value, share = solve(level, value, True, level == 0, arrived=arrived)
    return value


def solution(mesh):
    return jax.shard_map(
        local,
        mesh=mesh,
        in_specs=(
            P("layer", None, None, "front"),
            P("layer", None, "front", None),
            P("layer", None, "front", None),
            P("layer", None, "front", None),
            P("layer", None, None, "front"),
            P("layer", None, "front", None),
            P("layer", None, "front", None),
            P("layer", None),
        ),
        out_specs=P("layer", None, None, "front"),
        check_vma=False,
    )
```

```python
import jax
import jax.numpy as jnp
from jax import lax
from jax.experimental import pallas as pl
from jax.experimental.pallas import tpu as pltpu
from jax.sharding import PartitionSpec as P

FEW_CHIPS = 8
BF16, F32 = jnp.bfloat16, jnp.float32
VMEM = pl.BlockSpec(memory_space=pltpu.VMEM)
SMEM = pl.BlockSpec(memory_space=pltpu.SMEM)
ANY = pl.BlockSpec(memory_space=pl.ANY)
MIB = 2**20


def xor_route(axis, distance):
    return [(i, i ^ distance) for i in range(lax.axis_size(axis))]


def pair(block):
    return lax.ppermute(block, "front", xor_route("front", 1))


def same_core_groups():
    slots = lax.axis_size("front")
    return [list(range(core, slots, 2)) for core in range(2)]


def arrival_order(chip, chips):
    steps = jnp.arange(chips, dtype=jnp.int32)
    return chip ^ ((chips - steps) % chips) if chips <= FEW_CHIPS else steps


def from_chips(block, chips):
    return [block] + [
        lax.ppermute(block, "front", xor_route("front", 2 * (chips - step)))
        for step in range(1, chips)
    ]


def gather_chips(block, after=None):
    chips = lax.axis_size("front") // 2
    if chips > FEW_CHIPS:
        groups = same_core_groups()
        return lax.all_gather(block, "front", axis=1, tiled=True, axis_index_groups=groups)
    parts = from_chips(block, chips)
    if after is None:
        return jnp.concatenate(parts, axis=1)
    return join_parts(parts, after)


def hop(block, source_layer, target_layer):
    slots = lax.axis_size("front")
    others = [i for i in range(lax.axis_size("layer")) if i not in (source_layer, target_layer)]
    order = [source_layer, target_layer] + others
    target = dict(zip(order, order[1:] + order[:1]))
    return [
        lax.ppermute(
            block,
            ("layer", "front"),
            [(i * slots + j, target[i] * slots + (j ^ cross)) for i in target for j in range(slots)],
        )
        for cross in range(2)
    ]


def sum_chips(block, after=None):
    chips = lax.axis_size("front") // 2
    if chips > FEW_CHIPS:
        groups = same_core_groups()
        return lax.psum(block.astype(F32), "front", axis_index_groups=groups).astype(BF16)
    parts = from_chips(block, chips)
    if after is None:
        return sum(part.astype(F32) for part in parts).astype(BF16)
    return add_parts(parts, after)


def in_vmem(block):
    return pltpu.with_memory_space_constraint(block, pltpu.VMEM)


def in_hbm(block):
    return pltpu.with_memory_space_constraint(block, pltpu.HBM)


def params(mib):
    return pltpu.CompilerParams(vmem_limit_bytes=mib * MIB)


def cost(flops, nbytes):
    return pl.CostEstimate(flops=flops, bytes_accessed=nbytes, transcendentals=0)


def turned(vector):
    count = vector.shape[0] // 2
    return jnp.concatenate([-vector[count:], vector[:count]], axis=0)


def operands(vector):
    return vector.astype(BF16), turned(vector).astype(BF16)


def times(vector, real_matrix, imag_matrix, contract):
    straight, cross = operands(vector)
    dims = (((1,), (contract,)), ((), ()))
    return lax.dot_general(
        straight, real_matrix, dims, preferred_element_type=F32
    ) + lax.dot_general(cross, imag_matrix, dims, preferred_element_type=F32)


def transpose_sep(sep, after):
    _, rows, total = sep.shape
    step = 128 if rows % 128 == 0 else rows
    chunks = [(part, at) for part in range(2) for at in range(0, rows, step)]

    def kernel(sep_ref, _, out, stored, done):
        copies = []
        for index, (part, at) in enumerate(chunks):
            piece = (part, pl.ds(at, step))
            copy = pltpu.make_async_copy(sep_ref.at[piece], stored.at[piece], done.at[index])
            copy.start()
            copies.append(copy)
        for copy, (part, at) in zip(copies, chunks):
            copy.wait()
            out[part, :, pl.ds(at, step)] = stored[part, pl.ds(at, step), :].T

    return pl.pallas_call(
        kernel,
        in_specs=[ANY, ANY],
        out_specs=VMEM,
        out_shape=pltpu.VMEM((2, total, rows), BF16),
        scratch_shapes=[pltpu.VMEM(sep.shape, BF16), pltpu.SemaphoreType.DMA((len(chunks),))],
        compiler_params=params(18),
        cost_estimate=cost(0, 4 * sep.size),
        name="transpose_sep",
    )(in_hbm(sep), after)


def hold(blocks, after):
    def kernel(*refs):
        del refs

    return pl.pallas_call(
        kernel,
        in_specs=[ANY] * (len(blocks) + 1),
        out_specs=[ANY] * len(blocks),
        out_shape=[jax.ShapeDtypeStruct(block.shape, block.dtype) for block in blocks],
        input_output_aliases={index: index for index in range(len(blocks))},
        compiler_params=params(1),
        name="hold",
    )(*blocks, after)


def transpose_gather(own, theirs, after):
    _, total, cells = own.shape
    half = total // 2
    step = 512

    def kernel(own_ref, theirs_ref, _, out):
        start = (lax.axis_index("front") % 2) * half
        for side, block in enumerate((own_ref, theirs_ref)):
            for part in range(2):
                for at in range(0, half, step):
                    rows = pl.ds(pl.multiple_of(start + at, step), step)
                    out[part, pl.ds(side * cells, cells), pl.ds(at, step)] = block[part, rows, :].T

    return pl.pallas_call(
        kernel,
        in_specs=[VMEM, VMEM, ANY],
        out_specs=VMEM,
        out_shape=pltpu.VMEM((2, 2 * cells, half), BF16),
        compiler_params=params(16),
        cost_estimate=cost(0, 4 * own.size),
        name="transpose_gather",
    )(in_vmem(own), in_vmem(theirs), after)


def panel_columns(owner_ref, step, rows):
    slots = owner_ref.shape[0]
    place = lax.axis_index("front")
    chips = slots // 2
    chip = place // 2 ^ ((chips - step) % chips) if chips <= FEW_CHIPS else step
    panel = jnp.int32(0)
    for at in range(1, slots):
        panel = jnp.where(owner_ref[at] == 2 * chip + place % 2, at, panel)
    return pl.ds(pl.multiple_of(panel * rows, 128), rows)


def transpose_maps(own, theirs, owner, rows, after):
    _, cells, width = own.shape
    slots = owner.shape[0]
    chips = slots // 2

    def kernel(owner_ref, own_ref, theirs_ref, _, out, blocks_out):
        for step in range(chips):
            columns = panel_columns(owner_ref, step, rows)
            for side, block in enumerate((own_ref, theirs_ref)):
                for part in range(2):
                    out[part, pl.ds(step * rows, rows), pl.ds(side * cells, cells)] = block[
                        part, :, columns
                    ].T
        for side, block in enumerate((own_ref, theirs_ref)):
            for kind in range(3):
                columns = pl.ds(slots * rows + kind * cells, cells)
                for part in range(2):
                    blocks_out[side, kind, part] = block[part, :, columns]

    return pl.pallas_call(
        kernel,
        in_specs=[SMEM, VMEM, VMEM, ANY],
        out_specs=[VMEM, VMEM],
        out_shape=[
            pltpu.VMEM((2, chips * rows, 2 * cells), BF16),
            jax.ShapeDtypeStruct((2, 3, 2, cells, cells), BF16),
        ],
        compiler_params=params(16),
        cost_estimate=cost(0, 4 * own.size),
        name="transpose_maps",
    )(owner, in_vmem(own), in_vmem(theirs), after)


def take_maps(own, theirs, owner, rows):
    _, cells, width = own.shape
    slots = owner.shape[0]
    total = slots * rows
    place = lax.axis_index("front")
    slot_ids = jnp.arange(slots, dtype=jnp.int32)
    panel_of = jnp.sum(jnp.where(owner[None, :] == slot_ids[:, None], slot_ids[None, :], 0), axis=1)
    wanted = panel_of[2 * arrival_order(place // 2, slots // 2) + place % 2]

    def columns(maps):
        chosen = jnp.take(maps[:, :, :total].reshape(2, cells, slots, rows), wanted, axis=2)
        return jnp.swapaxes(chosen.reshape(2, cells, total // 2), 1, 2)

    def blocks(maps):
        return jnp.moveaxis(maps[:, :, total:].reshape(2, cells, 3, cells), 2, 0)

    spread = jnp.concatenate([columns(own), columns(theirs)], axis=2)
    return spread, jnp.stack([blocks(own), blocks(theirs)])


def add_parts(parts, after):
    def kernel(*refs):
        out = refs[-1]
        total = refs[0][...].astype(F32)
        for part in refs[1 : len(parts)]:
            total = total + part[...].astype(F32)
        out[...] = total.astype(BF16)

    return pl.pallas_call(
        kernel,
        in_specs=[VMEM] * len(parts) + [ANY],
        out_specs=VMEM,
        out_shape=jax.ShapeDtypeStruct(parts[0].shape, BF16),
        compiler_params=params(16),
        cost_estimate=cost(4 * parts[0].size, 10 * parts[0].size),
        name="add_parts",
    )(*parts, in_vmem(after))


def join_parts(parts, after):
    width = parts[0].shape[1]

    def kernel(*refs):
        out = refs[-1]
        for index, part in enumerate(refs[: len(parts)]):
            out[:, pl.ds(index * width, width)] = part[...]

    return pl.pallas_call(
        kernel,
        in_specs=[VMEM] * len(parts) + [ANY],
        out_specs=VMEM,
        out_shape=jax.ShapeDtypeStruct((8, len(parts) * width), BF16),
        compiler_params=params(16),
        cost_estimate=cost(0, 8 * parts[0].size),
        name="join_parts",
    )(*parts, in_vmem(after))


def first_leaf_and_gather(sources, gather, maps):
    cells = gather.shape[2]
    half = gather.shape[1] // 2
    starts = [sum(block.shape[2] for block in maps[:index]) for index in range(len(maps))]
    width = sum(block.shape[2] for block in maps)

    def kernel(*refs):
        sources_hbm, gather_hbm, *maps_hbm = refs[: 2 + len(maps)]
        keep, give, gather_ref, maps_ref, sources_ref, done = refs[2 + len(maps) :]
        core = lax.axis_index("front") % 2
        layer = lax.axis_index("layer")
        sides = [pl.ds(pl.multiple_of(side * half, half), half) for side in (1 - core, core)]
        leaf_at = pl.ds(starts[1], cells)
        values_at, sources_at = pl.ds(half, cells), pl.ds(half + cells, cells)
        pieces = [(sources_hbm, sources_ref), (maps_hbm[1], maps_ref.at[:, :, leaf_at])]
        for rows in sides:
            for part in range(2):
                pieces.append((gather_hbm.at[part, rows], gather_ref.at[part, rows]))
        for index in (0, 2, 3):
            columns = pl.ds(starts[index], maps[index].shape[2])
            pieces.append((maps_hbm[index], maps_ref.at[:, :, columns]))
        copies = [
            pltpu.make_async_copy(source, target, done.at[index])
            for index, (source, target) in enumerate(pieces)
        ]
        for copy in copies:
            copy.start()
        copies[0].wait()
        copies[1].wait()
        source = jnp.concatenate([sources_ref[0], sources_ref[1]], axis=0)
        for out in (give, keep):
            out[:, sources_at] = source

        @pl.when(layer == 0)
        def _():
            leaf_values = times(source, maps_ref[0, :, leaf_at], maps_ref[1, :, leaf_at], 1)
            for out in (give, keep):
                out[:, values_at] = leaf_values

        for index, (out, rows) in enumerate(zip((give, keep), sides)):
            copies[2 + 2 * index].wait()
            copies[3 + 2 * index].wait()

            @pl.when(layer == 0)
            def _(out=out, rows=rows):
                leaf_values = out[:, values_at]
                out[:, pl.ds(0, half)] = times(
                    leaf_values, gather_ref[0, rows, :], gather_ref[1, rows, :], 1
                )

        for copy in copies[6:]:
            copy.wait()

    return pl.pallas_call(
        kernel,
        in_specs=[ANY] * (2 + len(maps)),
        out_specs=[VMEM] * 4,
        out_shape=[
            jax.ShapeDtypeStruct((8, half + 2 * cells), F32),
            jax.ShapeDtypeStruct((8, half + 2 * cells), F32),
            pltpu.VMEM(gather.shape, BF16),
            pltpu.VMEM((2, cells, width), BF16),
        ],
        scratch_shapes=[pltpu.VMEM(sources.shape, F32), pltpu.SemaphoreType.DMA((9,))],
        compiler_params=params(16),
        cost_estimate=cost(16 * gather.size, 2 * gather.size),
        name="first_leaf_and_gather",
    )(in_hbm(sources), in_hbm(gather), *[in_hbm(block) for block in maps])


def leaf_and_gather(level, blocks, gather, arrived, sources=None):
    cells = blocks.shape[3]
    width = gather.shape[2]
    given = list(arrived) if sources is None else [*arrived, sources]

    def kernel(*refs):
        blocks_ref, gather_ref, leaf_out, sums_out = refs[-4:]

        def apply(vector, kind):
            return jnp.concatenate(
                [
                    times(
                        vector[:, side * cells : (side + 1) * cells],
                        blocks_ref[side, kind, 0],
                        blocks_ref[side, kind, 1],
                        1,
                    )
                    for side in range(2)
                ],
                axis=1,
            )

        @pl.when(lax.axis_index("layer") == level)
        def _():
            crossed = jnp.concatenate([refs[1][:, cells:], refs[1][:, :cells]], axis=1)
            source = apply(refs[0][...] + crossed, 2 if sources is None else 1)
            if sources is not None:
                source = refs[2][...] - source
            leaf_values = apply(source, 0)
            leaf_out[...] = leaf_values
            sums_out[...] = times(leaf_values, gather_ref[0], gather_ref[1], 0).astype(BF16)

    return pl.pallas_call(
        kernel,
        in_specs=[VMEM] * (len(given) + 2),
        out_specs=[VMEM, VMEM],
        out_shape=[
            jax.ShapeDtypeStruct((8, 2 * cells), F32),
            jax.ShapeDtypeStruct((8, width), BF16),
        ],
        compiler_params=params(16),
        cost_estimate=cost(32 * gather.size, 2 * gather.size),
        name="leaf_and_gather",
    )(*given, blocks, in_vmem(gather))


def folded(blocks, gather, kind, layers, after):
    cells = blocks.shape[3]

    def kernel(blocks_ref, gather_ref, _, out):
        layer = lax.axis_index("layer")

        @pl.when(jnp.logical_and(layer >= layers[0], layer <= layers[-1]))
        def _():
            for side in range(2):
                left = [blocks_ref[side, 0, part] for part in range(2)]
                right = [blocks_ref[side, kind, part] for part in range(2)]

                def product(i, j, left=left, right=right):
                    return jnp.dot(left[i], right[j], preferred_element_type=F32)

                real = (product(0, 0) - product(1, 1)).T
                imag = (product(0, 1) + product(1, 0)).T
                at = pl.ds(side * cells, cells)
                maps = [gather_ref[part, at, :] for part in range(2)]

                def applied(matrix, part, maps=maps):
                    return jnp.dot(matrix.astype(BF16), maps[part], preferred_element_type=F32)

                out[0, at, :] = (applied(real, 0) - applied(imag, 1)).astype(BF16)
                out[1, at, :] = (applied(real, 1) + applied(imag, 0)).astype(BF16)

    return pl.pallas_call(
        kernel,
        in_specs=[VMEM, VMEM, ANY],
        out_specs=VMEM,
        out_shape=pltpu.VMEM(gather.shape, BF16),
        compiler_params=params(20),
        cost_estimate=cost(8 * cells * gather.size, 4 * gather.size),
        name="folded",
    )(blocks, in_vmem(gather), after)


def block_products(vector, blocks_ref, kind):
    cells = blocks_ref.shape[3]
    return jnp.concatenate(
        [
            times(
                vector[:, side * cells : (side + 1) * cells],
                blocks_ref[side, kind, 0],
                blocks_ref[side, kind, 1],
                1,
            )
            for side in range(2)
        ],
        axis=1,
    )


def source_sums(blocks, gather, sources, layers):
    def kernel(blocks_ref, gather_ref, sources_ref, leaf_out, sums_out):
        layer = lax.axis_index("layer")

        @pl.when(jnp.logical_and(layer >= layers[0], layer <= layers[-1]))
        def _():
            leaf_values = block_products(sources_ref[...], blocks_ref, 0)
            leaf_out[...] = leaf_values
            sums_out[...] = times(leaf_values, gather_ref[0], gather_ref[1], 0)

    return pl.pallas_call(
        kernel,
        in_specs=[VMEM] * 3,
        out_specs=[VMEM] * 2,
        out_shape=[
            jax.ShapeDtypeStruct(sources.shape, F32),
            jax.ShapeDtypeStruct((8, gather.shape[2]), F32),
        ],
        compiler_params=params(16),
        cost_estimate=cost(32 * gather.size, 2 * gather.size),
        name="source_sums",
    )(blocks, in_vmem(gather), sources)


def folded_sums(level, arrived, fold, own_sums=None):
    given = [*arrived] if own_sums is None else [*arrived, own_sums]

    def kernel(*refs):
        fold_ref, out = refs[-2:]
        cells = refs[0].shape[1] // 2

        @pl.when(lax.axis_index("layer") == level)
        def _():
            crossed = jnp.concatenate([refs[1][:, cells:], refs[1][:, :cells]], axis=1)
            sums = times(refs[0][...] + crossed, fold_ref[0], fold_ref[1], 0)
            if own_sums is not None:
                sums = refs[2][...] - sums
            out[...] = sums.astype(BF16)

    return pl.pallas_call(
        kernel,
        in_specs=[VMEM] * (len(given) + 1),
        out_specs=VMEM,
        out_shape=jax.ShapeDtypeStruct((8, fold.shape[2]), BF16),
        compiler_params=params(16),
        cost_estimate=cost(32 * fold.size, 2 * fold.size),
        name="folded_sums",
    )(*given, in_vmem(fold))


def leaf_only(level, arrived, blocks, own_values=None):
    given = [*arrived] if own_values is None else [*arrived, own_values]

    def kernel(*refs):
        blocks_ref, out = refs[-2:]
        cells = blocks_ref.shape[3]

        @pl.when(lax.axis_index("layer") == level)
        def _():
            crossed = jnp.concatenate([refs[1][:, cells:], refs[1][:, :cells]], axis=1)
            kind = 2 if own_values is None else 1
            coupled = block_products(refs[0][...] + crossed, blocks_ref, kind)
            value = block_products(coupled, blocks_ref, 0)
            out[...] = value if own_values is None else refs[2][...] - value

    return pl.pallas_call(
        kernel,
        in_specs=[VMEM] * (len(given) + 1),
        out_specs=VMEM,
        out_shape=jax.ShapeDtypeStruct(arrived[0].shape, F32),
        compiler_params=params(16),
        cost_estimate=cost(16 * blocks.size, 2 * blocks.size),
        name="leaf_only",
    )(*given, blocks)


def sep_rows(level, sums, sep, other, before=None):
    half = sums.shape[1]
    rows = sep.shape[2]
    given = [sums] if before is None else [sums, before]

    def kernel(*refs):
        sums_ref, sep_ref, out = refs[0], refs[len(given)], refs[-1]

        @pl.when(lax.axis_index("layer") == level)
        def _():
            core = lax.axis_index("front") % 2
            side = 1 - core if other else core
            at = pl.ds(pl.multiple_of(side * half, half), half)
            value = times(sums_ref[...].astype(F32), sep_ref[0, at, :], sep_ref[1, at, :], 0)
            if before is not None:
                value = value + refs[1][...]
            out[...] = value.astype(out.dtype)

    return pl.pallas_call(
        kernel,
        in_specs=[VMEM] * (len(given) + 1),
        out_specs=VMEM,
        out_shape=jax.ShapeDtypeStruct((8, rows), F32 if before is None else BF16),
        compiler_params=params(16),
        cost_estimate=cost(16 * sep.size, sep.size),
        name="sep_rows",
    )(*given, in_vmem(sep))


def share_of_value(part, leaf_values, before, subtract):
    first = jnp.where(lax.axis_index("front") % 2 == 0, 1.0, 0.0)
    if subtract:
        return first * (before - leaf_values) + part
    return first * leaf_values - part


def spread_cells(level, stored, spread, leaf_values, before=None, subtract=False, last=False):
    given = [stored, leaf_values] + ([before] if subtract else [])
    outputs = 1 if last else 2

    def kernel(*refs):
        stored_ref, leaf_ref = refs[:2]
        spread_ref, part_out = refs[-1 - outputs], refs[-outputs]

        @pl.when(lax.axis_index("layer") == level)
        def _():
            part = times(stored_ref[...].astype(F32), spread_ref[0], spread_ref[1], 0)
            part_out[...] = part
            if not last:
                held = refs[2][...] if subtract else None
                refs[-1][...] = share_of_value(part, leaf_ref[...], held, subtract)

    return pl.pallas_call(
        kernel,
        in_specs=[VMEM] * (len(given) + 1),
        out_specs=[VMEM] * outputs,
        out_shape=[jax.ShapeDtypeStruct((8, spread.shape[2]), F32)] * outputs,
        compiler_params=params(16),
        cost_estimate=cost(32 * spread.size, 2 * spread.size),
        name="spread_cells",
    )(*given, in_vmem(spread))


def finish(level, leaf_values, part, theirs, before=None, subtract=False, last=False):
    cells = part.shape[1] // 2
    given = [leaf_values, part, theirs] + ([] if before is None else [before])

    def kernel(*refs):
        leaf_ref, part_ref, theirs_ref = refs[:3]
        here = lax.axis_index("layer") == level

        def store(value):
            if last:
                refs[-1][0, 0] = value[:4, :cells]
                refs[-1][0, 1] = value[4:, :cells]
            else:
                refs[-1][...] = value

        @pl.when(here)
        def _():
            swapped = jnp.concatenate([theirs_ref[:, cells:], theirs_ref[:, :cells]], axis=1)
            solved = leaf_ref[...] - (part_ref[...] + swapped)
            if subtract:
                solved = refs[3][...] - solved
            store(solved)

        if before is not None:

            @pl.when(jnp.logical_not(here))
            def _():
                store(refs[3][...])

    return pl.pallas_call(
        kernel,
        in_specs=[VMEM] * len(given),
        out_specs=VMEM,
        out_shape=jax.ShapeDtypeStruct((1, 2, 4, cells) if last else part.shape, F32),
        compiler_params=params(16),
        cost_estimate=cost(4 * part.size, 16 * part.size),
        name="finish",
    )(*given)


def local(
    right_sides,
    leaf_inverse,
    couple_above,
    couple_below,
    sep_gather,
    sep_inverse,
    sep_spread,
    panel_owner,
):
    depth = lax.axis_size("layer")
    cells = leaf_inverse.shape[2]
    rows = sep_inverse.shape[2]

    maps = [sep_spread[0], leaf_inverse[0], couple_above[0], couple_below[0]]
    keep, give, own_gather, own_maps = first_leaf_and_gather(right_sides[0], sep_gather[0], maps)
    got = pair(give)
    half = sep_gather.shape[2] // 2
    first_sums = (keep[:, :half] + got[:, :half]).astype(BF16)
    first_values, sources = (
        jnp.concatenate([block[:, at : at + cells] for block in (keep, got)], axis=1)
        for at in (half, half + cells)
    )

    own_gather, own_maps = hold([own_gather, own_maps], first_sums)
    their_gather, their_maps = pair(own_gather), pair(own_maps)
    sep = transpose_sep(sep_inverse[0], first_sums)

    def own_rows_of(level, half_sums):
        other_sums = pair(half_sums)
        own_rows = sep_rows(level, half_sums, sep, False)
        return sep_rows(level, other_sums, sep, True, own_rows)

    def solve(level, before, subtract=False, last=False, arrived=None):
        if subtract:
            sums = folded_sums(level, arrived, fold_below)
            leaf_values = leaf_only(level, arrived, blocks)
        elif level > 1:
            sums = folded_sums(level, arrived, fold_above, source_parts[1])
            leaf_values = leaf_only(level, arrived, blocks, source_parts[0])
        else:
            leaf_values, sums = leaf_and_gather(level, blocks, gather, arrived, sources)
        stored = gather_chips(own_rows_of(level, sum_chips(sums, leaf_values)))
        part, *share = spread_cells(level, stored, spread, leaf_values, before, subtract, last)
        return finish(level, leaf_values, part, pair(part), before, subtract, last), *share

    own_rows = own_rows_of(0, sum_chips(first_sums, sep))
    if rows % 128 == 0:
        spread, blocks = transpose_maps(own_maps, their_maps, panel_owner[0], rows, own_rows)
    else:
        spread, blocks = take_maps(own_maps, their_maps, panel_owner[0], rows)
    part, share = spread_cells(0, gather_chips(own_rows, spread), spread, first_values)
    arrived = hop(share, 0, 1)
    value = finish(0, first_values, part, pair(part))
    gather = transpose_gather(own_gather, their_gather, share)

    fold_above = folded(blocks, gather, 1, range(2, depth), share)
    source_parts = source_sums(blocks, gather, sources, range(2, depth))

    for level in range(1, depth):
        if level > 1:
            arrived = hop(share, level - 1, level)
        value, share = solve(level, value, arrived=arrived)
        if level == depth - 2:
            fold_below = folded(blocks, gather, 2, range(depth - 1), share)
    for level in range(depth - 2, -1, -1):
        arrived = hop(share[0] if level < depth - 2 else share, level + 1, level)
        value, *share = solve(level, value, True, level == 0, arrived=arrived)
    return value


def solution(mesh):
    return jax.shard_map(
        local,
        mesh=mesh,
        in_specs=(
            P("layer", None, None, "front"),
            P("layer", None, "front", None),
            P("layer", None, "front", None),
            P("layer", None, "front", None),
            P("layer", None, None, "front"),
            P("layer", None, "front", None),
            P("layer", None, "front", None),
            P("layer", None),
        ),
        out_specs=P("layer", None, None, "front"),
        check_vma=False,
    )
```

```python
import jax
import jax.numpy as jnp
from jax import lax
from jax.experimental import pallas as pl
from jax.experimental.pallas import tpu as pltpu
from jax.sharding import PartitionSpec as P

FEW_CHIPS = 8
BF16, F32 = jnp.bfloat16, jnp.float32
VMEM = pl.BlockSpec(memory_space=pltpu.VMEM)
SMEM = pl.BlockSpec(memory_space=pltpu.SMEM)
ANY = pl.BlockSpec(memory_space=pl.ANY)
MIB = 2**20


def xor_route(axis, distance):
    return [(i, i ^ distance) for i in range(lax.axis_size(axis))]


def pair(block):
    return lax.ppermute(block, "front", xor_route("front", 1))


def same_core_groups():
    slots = lax.axis_size("front")
    return [list(range(core, slots, 2)) for core in range(2)]


def arrival_order(chip, chips):
    steps = jnp.arange(chips, dtype=jnp.int32)
    return chip ^ ((chips - steps) % chips) if chips <= FEW_CHIPS else steps


def from_chips(block, chips):
    return [block] + [
        lax.ppermute(block, "front", xor_route("front", 2 * (chips - step)))
        for step in range(1, chips)
    ]


def gather_chips(block, after=None):
    chips = lax.axis_size("front") // 2
    if chips > FEW_CHIPS:
        groups = same_core_groups()
        return lax.all_gather(block, "front", axis=1, tiled=True, axis_index_groups=groups)
    parts = from_chips(block, chips)
    if after is None:
        return jnp.concatenate(parts, axis=1)
    return join_parts(parts, after)


def hop(block, source_layer, target_layer):
    slots = lax.axis_size("front")
    others = [i for i in range(lax.axis_size("layer")) if i not in (source_layer, target_layer)]
    order = [source_layer, target_layer] + others
    target = dict(zip(order, order[1:] + order[:1]))
    return [
        lax.ppermute(
            block,
            ("layer", "front"),
            [(i * slots + j, target[i] * slots + (j ^ cross)) for i in target for j in range(slots)],
        )
        for cross in range(2)
    ]


def sum_chips(block, after=None):
    chips = lax.axis_size("front") // 2
    if chips > FEW_CHIPS:
        groups = same_core_groups()
        return lax.psum(block.astype(F32), "front", axis_index_groups=groups).astype(BF16)
    parts = from_chips(block, chips)
    if after is None:
        return sum(part.astype(F32) for part in parts).astype(BF16)
    return add_parts(parts, after)


def in_vmem(block):
    return pltpu.with_memory_space_constraint(block, pltpu.VMEM)


def in_hbm(block):
    return pltpu.with_memory_space_constraint(block, pltpu.HBM)


def params(mib):
    return pltpu.CompilerParams(vmem_limit_bytes=mib * MIB)


def cost(flops, nbytes):
    return pl.CostEstimate(flops=flops, bytes_accessed=nbytes, transcendentals=0)


def turned(vector):
    count = vector.shape[0] // 2
    return jnp.concatenate([-vector[count:], vector[:count]], axis=0)


def operands(vector):
    return vector.astype(BF16), turned(vector).astype(BF16)


def times(vector, real_matrix, imag_matrix, contract):
    straight, cross = operands(vector)
    dims = (((1,), (contract,)), ((), ()))
    return lax.dot_general(
        straight, real_matrix, dims, preferred_element_type=F32
    ) + lax.dot_general(cross, imag_matrix, dims, preferred_element_type=F32)


def transpose_sep(sep, after):
    _, rows, total = sep.shape
    step = 128 if rows % 128 == 0 else rows
    chunks = [(part, at) for part in range(2) for at in range(0, rows, step)]

    def kernel(sep_ref, _, out, stored, done):
        copies = []
        for index, (part, at) in enumerate(chunks):
            piece = (part, pl.ds(at, step))
            copy = pltpu.make_async_copy(sep_ref.at[piece], stored.at[piece], done.at[index])
            copy.start()
            copies.append(copy)
        for copy, (part, at) in zip(copies, chunks):
            copy.wait()
            out[part, :, pl.ds(at, step)] = stored[part, pl.ds(at, step), :].T

    return pl.pallas_call(
        kernel,
        in_specs=[ANY, ANY],
        out_specs=VMEM,
        out_shape=pltpu.VMEM((2, total, rows), BF16),
        scratch_shapes=[pltpu.VMEM(sep.shape, BF16), pltpu.SemaphoreType.DMA((len(chunks),))],
        compiler_params=params(18),
        cost_estimate=cost(0, 4 * sep.size),
        name="transpose_sep",
    )(in_hbm(sep), after)


def hold(blocks, after):
    def kernel(*refs):
        del refs

    return pl.pallas_call(
        kernel,
        in_specs=[ANY] * (len(blocks) + 1),
        out_specs=[ANY] * len(blocks),
        out_shape=[jax.ShapeDtypeStruct(block.shape, block.dtype) for block in blocks],
        input_output_aliases={index: index for index in range(len(blocks))},
        compiler_params=params(1),
        name="hold",
    )(*blocks, after)


def transpose_gather(own, theirs, after):
    _, total, cells = own.shape
    half = total // 2
    step = 512

    def kernel(own_ref, theirs_ref, _, out):
        start = (lax.axis_index("front") % 2) * half
        for side, block in enumerate((own_ref, theirs_ref)):
            for part in range(2):
                for at in range(0, half, step):
                    rows = pl.ds(pl.multiple_of(start + at, step), step)
                    out[part, pl.ds(side * cells, cells), pl.ds(at, step)] = block[part, rows, :].T

    return pl.pallas_call(
        kernel,
        in_specs=[VMEM, VMEM, ANY],
        out_specs=VMEM,
        out_shape=pltpu.VMEM((2, 2 * cells, half), BF16),
        compiler_params=params(16),
        cost_estimate=cost(0, 4 * own.size),
        name="transpose_gather",
    )(in_vmem(own), in_vmem(theirs), after)


def panel_columns(owner_ref, step, rows):
    slots = owner_ref.shape[0]
    place = lax.axis_index("front")
    chips = slots // 2
    chip = place // 2 ^ ((chips - step) % chips) if chips <= FEW_CHIPS else step
    panel = jnp.int32(0)
    for at in range(1, slots):
        panel = jnp.where(owner_ref[at] == 2 * chip + place % 2, at, panel)
    return pl.ds(pl.multiple_of(panel * rows, 128), rows)


def transpose_maps(own, theirs, owner, rows, after):
    _, cells, width = own.shape
    slots = owner.shape[0]
    chips = slots // 2

    def kernel(owner_ref, own_ref, theirs_ref, _, out, blocks_out):
        for step in range(chips):
            columns = panel_columns(owner_ref, step, rows)
            for side, block in enumerate((own_ref, theirs_ref)):
                for part in range(2):
                    out[part, pl.ds(step * rows, rows), pl.ds(side * cells, cells)] = block[
                        part, :, columns
                    ].T
        for side, block in enumerate((own_ref, theirs_ref)):
            for kind in range(3):
                columns = pl.ds(slots * rows + kind * cells, cells)
                for part in range(2):
                    blocks_out[side, kind, part] = block[part, :, columns]

    return pl.pallas_call(
        kernel,
        in_specs=[SMEM, VMEM, VMEM, ANY],
        out_specs=[VMEM, VMEM],
        out_shape=[
            pltpu.VMEM((2, chips * rows, 2 * cells), BF16),
            jax.ShapeDtypeStruct((2, 3, 2, cells, cells), BF16),
        ],
        compiler_params=params(16),
        cost_estimate=cost(0, 4 * own.size),
        name="transpose_maps",
    )(owner, in_vmem(own), in_vmem(theirs), after)


def take_maps(own, theirs, owner, rows):
    _, cells, width = own.shape
    slots = owner.shape[0]
    total = slots * rows
    place = lax.axis_index("front")
    slot_ids = jnp.arange(slots, dtype=jnp.int32)
    panel_of = jnp.sum(jnp.where(owner[None, :] == slot_ids[:, None], slot_ids[None, :], 0), axis=1)
    wanted = panel_of[2 * arrival_order(place // 2, slots // 2) + place % 2]

    def columns(maps):
        chosen = jnp.take(maps[:, :, :total].reshape(2, cells, slots, rows), wanted, axis=2)
        return jnp.swapaxes(chosen.reshape(2, cells, total // 2), 1, 2)

    def blocks(maps):
        return jnp.moveaxis(maps[:, :, total:].reshape(2, cells, 3, cells), 2, 0)

    spread = jnp.concatenate([columns(own), columns(theirs)], axis=2)
    return spread, jnp.stack([blocks(own), blocks(theirs)])


def add_parts(parts, after):
    def kernel(*refs):
        out = refs[-1]
        total = refs[0][...].astype(F32)
        for part in refs[1 : len(parts)]:
            total = total + part[...].astype(F32)
        out[...] = total.astype(BF16)

    return pl.pallas_call(
        kernel,
        in_specs=[VMEM] * len(parts) + [ANY],
        out_specs=VMEM,
        out_shape=jax.ShapeDtypeStruct(parts[0].shape, BF16),
        compiler_params=params(16),
        cost_estimate=cost(4 * parts[0].size, 10 * parts[0].size),
        name="add_parts",
    )(*parts, in_vmem(after))


def join_parts(parts, after):
    width = parts[0].shape[1]

    def kernel(*refs):
        out = refs[-1]
        for index, part in enumerate(refs[: len(parts)]):
            out[:, pl.ds(index * width, width)] = part[...]

    return pl.pallas_call(
        kernel,
        in_specs=[VMEM] * len(parts) + [ANY],
        out_specs=VMEM,
        out_shape=jax.ShapeDtypeStruct((8, len(parts) * width), BF16),
        compiler_params=params(16),
        cost_estimate=cost(0, 8 * parts[0].size),
        name="join_parts",
    )(*parts, in_vmem(after))


def first_leaf_and_gather(sources, gather, maps):
    cells = gather.shape[2]
    half = gather.shape[1] // 2
    starts = [sum(block.shape[2] for block in maps[:index]) for index in range(len(maps))]
    width = sum(block.shape[2] for block in maps)

    def kernel(*refs):
        sources_hbm, gather_hbm, *maps_hbm = refs[: 2 + len(maps)]
        keep, give, gather_ref, maps_ref, sources_ref, done = refs[2 + len(maps) :]
        core = lax.axis_index("front") % 2
        layer = lax.axis_index("layer")
        sides = [pl.ds(pl.multiple_of(side * half, half), half) for side in (1 - core, core)]
        leaf_at = pl.ds(starts[1], cells)
        values_at, sources_at = pl.ds(half, cells), pl.ds(half + cells, cells)
        pieces = [(sources_hbm, sources_ref), (maps_hbm[1], maps_ref.at[:, :, leaf_at])]
        for rows in sides:
            for part in range(2):
                pieces.append((gather_hbm.at[part, rows], gather_ref.at[part, rows]))
        for index in (0, 2, 3):
            columns = pl.ds(starts[index], maps[index].shape[2])
            pieces.append((maps_hbm[index], maps_ref.at[:, :, columns]))
        copies = [
            pltpu.make_async_copy(source, target, done.at[index])
            for index, (source, target) in enumerate(pieces)
        ]
        for copy in copies:
            copy.start()
        copies[0].wait()
        copies[1].wait()
        source = jnp.concatenate([sources_ref[0], sources_ref[1]], axis=0)
        for out in (give, keep):
            out[:, sources_at] = source

        @pl.when(layer == 0)
        def _():
            leaf_values = times(source, maps_ref[0, :, leaf_at], maps_ref[1, :, leaf_at], 1)
            for out in (give, keep):
                out[:, values_at] = leaf_values

        for index, (out, rows) in enumerate(zip((give, keep), sides)):
            copies[2 + 2 * index].wait()
            copies[3 + 2 * index].wait()

            @pl.when(layer == 0)
            def _(out=out, rows=rows):
                leaf_values = out[:, values_at]
                out[:, pl.ds(0, half)] = times(
                    leaf_values, gather_ref[0, rows, :], gather_ref[1, rows, :], 1
                )

        for copy in copies[6:]:
            copy.wait()

    return pl.pallas_call(
        kernel,
        in_specs=[ANY] * (2 + len(maps)),
        out_specs=[VMEM] * 4,
        out_shape=[
            jax.ShapeDtypeStruct((8, half + 2 * cells), F32),
            jax.ShapeDtypeStruct((8, half + 2 * cells), F32),
            pltpu.VMEM(gather.shape, BF16),
            pltpu.VMEM((2, cells, width), BF16),
        ],
        scratch_shapes=[pltpu.VMEM(sources.shape, F32), pltpu.SemaphoreType.DMA((9,))],
        compiler_params=params(16),
        cost_estimate=cost(16 * gather.size, 2 * gather.size),
        name="first_leaf_and_gather",
    )(in_hbm(sources), in_hbm(gather), *[in_hbm(block) for block in maps])


def leaf_and_gather(level, blocks, gather, arrived, sources=None):
    cells = blocks.shape[3]
    width = gather.shape[2]
    given = list(arrived) if sources is None else [*arrived, sources]

    def kernel(*refs):
        blocks_ref, gather_ref, leaf_out, sums_out = refs[-4:]

        def apply(vector, kind):
            return jnp.concatenate(
                [
                    times(
                        vector[:, side * cells : (side + 1) * cells],
                        blocks_ref[side, kind, 0],
                        blocks_ref[side, kind, 1],
                        1,
                    )
                    for side in range(2)
                ],
                axis=1,
            )

        @pl.when(lax.axis_index("layer") == level)
        def _():
            crossed = jnp.concatenate([refs[1][:, cells:], refs[1][:, :cells]], axis=1)
            source = apply(refs[0][...] + crossed, 2 if sources is None else 1)
            if sources is not None:
                source = refs[2][...] - source
            leaf_values = apply(source, 0)
            leaf_out[...] = leaf_values
            sums_out[...] = times(leaf_values, gather_ref[0], gather_ref[1], 0).astype(BF16)

    return pl.pallas_call(
        kernel,
        in_specs=[VMEM] * (len(given) + 2),
        out_specs=[VMEM, VMEM],
        out_shape=[
            jax.ShapeDtypeStruct((8, 2 * cells), F32),
            jax.ShapeDtypeStruct((8, width), BF16),
        ],
        compiler_params=params(16),
        cost_estimate=cost(32 * gather.size, 2 * gather.size),
        name="leaf_and_gather",
    )(*given, blocks, in_vmem(gather))


def folded(blocks, gather, kind, layers, after):
    cells = blocks.shape[3]

    def kernel(blocks_ref, gather_ref, _, out):
        layer = lax.axis_index("layer")

        @pl.when(jnp.logical_and(layer >= layers[0], layer <= layers[-1]))
        def _():
            for side in range(2):
                left = [blocks_ref[side, 0, part] for part in range(2)]
                right = [blocks_ref[side, kind, part] for part in range(2)]

                def product(i, j, left=left, right=right):
                    return jnp.dot(left[i], right[j], preferred_element_type=F32)

                real = (product(0, 0) - product(1, 1)).T
                imag = (product(0, 1) + product(1, 0)).T
                at = pl.ds(side * cells, cells)
                maps = [gather_ref[part, at, :] for part in range(2)]

                def applied(matrix, part, maps=maps):
                    return jnp.dot(matrix.astype(BF16), maps[part], preferred_element_type=F32)

                out[0, at, :] = (applied(real, 0) - applied(imag, 1)).astype(BF16)
                out[1, at, :] = (applied(real, 1) + applied(imag, 0)).astype(BF16)

    return pl.pallas_call(
        kernel,
        in_specs=[VMEM, VMEM, ANY],
        out_specs=VMEM,
        out_shape=pltpu.VMEM(gather.shape, BF16),
        compiler_params=params(20),
        cost_estimate=cost(8 * cells * gather.size, 4 * gather.size),
        name="folded",
    )(blocks, in_vmem(gather), after)


def block_products(vector, blocks_ref, kind):
    cells = blocks_ref.shape[3]
    return jnp.concatenate(
        [
            times(
                vector[:, side * cells : (side + 1) * cells],
                blocks_ref[side, kind, 0],
                blocks_ref[side, kind, 1],
                1,
            )
            for side in range(2)
        ],
        axis=1,
    )


def source_sums(blocks, gather, sources, layers):
    def kernel(blocks_ref, gather_ref, sources_ref, leaf_out, sums_out):
        layer = lax.axis_index("layer")

        @pl.when(jnp.logical_and(layer >= layers[0], layer <= layers[-1]))
        def _():
            leaf_values = block_products(sources_ref[...], blocks_ref, 0)
            leaf_out[...] = leaf_values
            sums_out[...] = times(leaf_values, gather_ref[0], gather_ref[1], 0)

    return pl.pallas_call(
        kernel,
        in_specs=[VMEM] * 3,
        out_specs=[VMEM] * 2,
        out_shape=[
            jax.ShapeDtypeStruct(sources.shape, F32),
            jax.ShapeDtypeStruct((8, gather.shape[2]), F32),
        ],
        compiler_params=params(16),
        cost_estimate=cost(32 * gather.size, 2 * gather.size),
        name="source_sums",
    )(blocks, in_vmem(gather), sources)


def folded_sums(level, arrived, fold, own_sums=None):
    given = [*arrived] if own_sums is None else [*arrived, own_sums]

    def kernel(*refs):
        fold_ref, out = refs[-2:]
        cells = refs[0].shape[1] // 2

        @pl.when(lax.axis_index("layer") == level)
        def _():
            crossed = jnp.concatenate([refs[1][:, cells:], refs[1][:, :cells]], axis=1)
            sums = times(refs[0][...] + crossed, fold_ref[0], fold_ref[1], 0)
            if own_sums is not None:
                sums = refs[2][...] - sums
            out[...] = sums.astype(BF16)

    return pl.pallas_call(
        kernel,
        in_specs=[VMEM] * (len(given) + 1),
        out_specs=VMEM,
        out_shape=jax.ShapeDtypeStruct((8, fold.shape[2]), BF16),
        compiler_params=params(16),
        cost_estimate=cost(32 * fold.size, 2 * fold.size),
        name="folded_sums",
    )(*given, in_vmem(fold))


def leaf_only(level, arrived, blocks, own_values=None):
    given = [*arrived] if own_values is None else [*arrived, own_values]

    def kernel(*refs):
        blocks_ref, out = refs[-2:]
        cells = blocks_ref.shape[3]

        @pl.when(lax.axis_index("layer") == level)
        def _():
            crossed = jnp.concatenate([refs[1][:, cells:], refs[1][:, :cells]], axis=1)
            kind = 2 if own_values is None else 1
            coupled = block_products(refs[0][...] + crossed, blocks_ref, kind)
            value = block_products(coupled, blocks_ref, 0)
            out[...] = value if own_values is None else refs[2][...] - value

    return pl.pallas_call(
        kernel,
        in_specs=[VMEM] * (len(given) + 1),
        out_specs=VMEM,
        out_shape=jax.ShapeDtypeStruct(arrived[0].shape, F32),
        compiler_params=params(16),
        cost_estimate=cost(16 * blocks.size, 2 * blocks.size),
        name="leaf_only",
    )(*given, blocks)


def sep_rows(level, sums, sep, other, before=None):
    half = sums.shape[1]
    rows = sep.shape[2]
    given = [sums] if before is None else [sums, before]

    def kernel(*refs):
        sums_ref, sep_ref, out = refs[0], refs[len(given)], refs[-1]

        @pl.when(lax.axis_index("layer") == level)
        def _():
            core = lax.axis_index("front") % 2
            side = 1 - core if other else core
            at = pl.ds(pl.multiple_of(side * half, half), half)
            value = times(sums_ref[...].astype(F32), sep_ref[0, at, :], sep_ref[1, at, :], 0)
            if before is not None:
                value = value + refs[1][...]
            out[...] = value.astype(out.dtype)

    return pl.pallas_call(
        kernel,
        in_specs=[VMEM] * (len(given) + 1),
        out_specs=VMEM,
        out_shape=jax.ShapeDtypeStruct((8, rows), F32 if before is None else BF16),
        compiler_params=params(16),
        cost_estimate=cost(16 * sep.size, sep.size),
        name="sep_rows",
    )(*given, in_vmem(sep))


def share_of_value(part, leaf_values, before, subtract):
    first = jnp.where(lax.axis_index("front") % 2 == 0, 1.0, 0.0)
    if subtract:
        return first * (before - leaf_values) + part
    return first * leaf_values - part


def spread_cells(level, stored, spread, leaf_values, held=(), before=None, last=False):
    given = [stored, leaf_values, *held] + ([] if before is None else [before])
    outputs = 2 if last else 3

    def kernel(*refs):
        stored_ref, leaf_ref = refs[:2]
        spread_ref = refs[len(given)]
        part_out, leaf_out = refs[len(given) + 1 : len(given) + 3]
        here = lax.axis_index("layer") == level

        @pl.when(here)
        def _():
            part = times(stored_ref[...].astype(F32), spread_ref[0], spread_ref[1], 0)
            part_out[...] = part
            leaf_out[...] = leaf_ref[...]
            if not last:
                value = None if before is None else refs[len(given) - 1][...]
                refs[-1][...] = share_of_value(part, leaf_ref[...], value, before is not None)

        if held:

            @pl.when(jnp.logical_not(here))
            def _():
                part_out[...] = refs[2][...]
                leaf_out[...] = refs[3][...]

    return pl.pallas_call(
        kernel,
        in_specs=[VMEM] * (len(given) + 1),
        out_specs=[VMEM] * outputs,
        out_shape=[jax.ShapeDtypeStruct((8, spread.shape[2]), F32)] * outputs,
        compiler_params=params(16),
        cost_estimate=cost(32 * spread.size, 2 * spread.size),
        name="spread_cells",
    )(*given, in_vmem(spread))


def finish(part, leaf_values, before=None, depth=0):
    cells = part.shape[1] // 2
    given = [leaf_values, part, pair(part)] + ([] if before is None else [before])

    def kernel(*refs):
        leaf_ref, part_ref, theirs_ref = refs[:3]
        swapped = jnp.concatenate([theirs_ref[:, cells:], theirs_ref[:, :cells]], axis=1)
        solved = leaf_ref[...] - (part_ref[...] + swapped)
        if before is None:
            refs[-1][...] = solved
        else:
            bottom = lax.axis_index("layer") == depth - 1
            value = refs[3][...] - jnp.where(bottom, 0.0, solved)
            refs[-1][0, 0] = value[:4, :cells]
            refs[-1][0, 1] = value[4:, :cells]

    return pl.pallas_call(
        kernel,
        in_specs=[VMEM] * len(given),
        out_specs=VMEM,
        out_shape=jax.ShapeDtypeStruct(part.shape if before is None else (1, 2, 4, cells), F32),
        compiler_params=params(16),
        cost_estimate=cost(4 * part.size, 16 * part.size),
        name="finish",
    )(*given)


def local(
    right_sides,
    leaf_inverse,
    couple_above,
    couple_below,
    sep_gather,
    sep_inverse,
    sep_spread,
    panel_owner,
):
    depth = lax.axis_size("layer")
    cells = leaf_inverse.shape[2]
    rows = sep_inverse.shape[2]

    maps = [sep_spread[0], leaf_inverse[0], couple_above[0], couple_below[0]]
    keep, give, own_gather, own_maps = first_leaf_and_gather(right_sides[0], sep_gather[0], maps)
    got = pair(give)
    half = sep_gather.shape[2] // 2
    first_sums = (keep[:, :half] + got[:, :half]).astype(BF16)
    first_values, sources = (
        jnp.concatenate([block[:, at : at + cells] for block in (keep, got)], axis=1)
        for at in (half, half + cells)
    )

    own_gather, own_maps = hold([own_gather, own_maps], first_sums)
    their_gather, their_maps = pair(own_gather), pair(own_maps)
    sep = transpose_sep(sep_inverse[0], first_sums)

    def own_rows_of(level, half_sums):
        other_sums = pair(half_sums)
        own_rows = sep_rows(level, half_sums, sep, False)
        return sep_rows(level, other_sums, sep, True, own_rows)

    def solve(level, arrived, held, before=None, last=False):
        if before is not None:
            sums = folded_sums(level, arrived, fold_below)
            leaf_values = leaf_only(level, arrived, blocks)
        elif level > 1:
            sums = folded_sums(level, arrived, fold_above, source_parts[1])
            leaf_values = leaf_only(level, arrived, blocks, source_parts[0])
        else:
            leaf_values, sums = leaf_and_gather(level, blocks, gather, arrived, sources)
        stored = gather_chips(own_rows_of(level, sum_chips(sums, leaf_values)))
        return spread_cells(level, stored, spread, leaf_values, held, before, last)

    own_rows = own_rows_of(0, sum_chips(first_sums, sep))
    if rows % 128 == 0:
        spread, blocks = transpose_maps(own_maps, their_maps, panel_owner[0], rows, own_rows)
    else:
        spread, blocks = take_maps(own_maps, their_maps, panel_owner[0], rows)
    *held, share = spread_cells(0, gather_chips(own_rows, spread), spread, first_values)
    arrived = hop(share, 0, 1)
    gather = transpose_gather(own_gather, their_gather, share)

    fold_above = folded(blocks, gather, 1, range(2, depth), share)
    source_parts = source_sums(blocks, gather, sources, range(2, depth))

    for level in range(1, depth):
        if level > 1:
            arrived = hop(share, level - 1, level)
        *held, share = solve(level, arrived, held)
        if level == depth - 2:
            fold_below = folded(blocks, gather, 2, range(depth - 1), share)
    value = finish(*held)
    for level in range(depth - 2, 0, -1):
        arrived = hop(share, level + 1, level)
        *held, share = solve(level, arrived, held, value)
    held = solve(0, hop(share, 1, 0), held, value, last=True)
    return finish(*held, value, depth)


def solution(mesh):
    return jax.shard_map(
        local,
        mesh=mesh,
        in_specs=(
            P("layer", None, None, "front"),
            P("layer", None, "front", None),
            P("layer", None, "front", None),
            P("layer", None, "front", None),
            P("layer", None, None, "front"),
            P("layer", None, "front", None),
            P("layer", None, "front", None),
            P("layer", None),
        ),
        out_specs=P("layer", None, None, "front"),
        check_vma=False,
    )
```

```python
import jax
import jax.numpy as jnp
from jax import lax
from jax.experimental import pallas as pl
from jax.experimental.pallas import tpu as pltpu
from jax.sharding import PartitionSpec as P

FEW_CHIPS = 8
BF16, F32 = jnp.bfloat16, jnp.float32
VMEM = pl.BlockSpec(memory_space=pltpu.VMEM)
SMEM = pl.BlockSpec(memory_space=pltpu.SMEM)
ANY = pl.BlockSpec(memory_space=pl.ANY)
MIB = 2**20


def xor_route(axis, distance):
    return [(i, i ^ distance) for i in range(lax.axis_size(axis))]


def pair(block):
    return lax.ppermute(block, "front", xor_route("front", 1))


def same_core_groups():
    slots = lax.axis_size("front")
    return [list(range(core, slots, 2)) for core in range(2)]


def arrival_order(chip, chips):
    steps = jnp.arange(chips, dtype=jnp.int32)
    return chip ^ ((chips - steps) % chips) if chips <= FEW_CHIPS else steps


def from_chips(block, chips):
    return [block] + [
        lax.ppermute(block, "front", xor_route("front", 2 * (chips - step)))
        for step in range(1, chips)
    ]


def gather_chips(block, after=None):
    chips = lax.axis_size("front") // 2
    if chips > FEW_CHIPS:
        groups = same_core_groups()
        return lax.all_gather(block, "front", axis=1, tiled=True, axis_index_groups=groups)
    parts = from_chips(block, chips)
    if after is None:
        return jnp.concatenate(parts, axis=1)
    return join_parts(parts, after)


def hop(block, source_layer, target_layer):
    slots = lax.axis_size("front")
    others = [i for i in range(lax.axis_size("layer")) if i not in (source_layer, target_layer)]
    order = [source_layer, target_layer] + others
    target = dict(zip(order, order[1:] + order[:1]))
    return [
        lax.ppermute(
            block,
            ("layer", "front"),
            [(i * slots + j, target[i] * slots + (j ^ cross)) for i in target for j in range(slots)],
        )
        for cross in range(2)
    ]


def sum_chips(block, after=None):
    chips = lax.axis_size("front") // 2
    if chips > FEW_CHIPS:
        groups = same_core_groups()
        return lax.psum(block.astype(F32), "front", axis_index_groups=groups).astype(BF16)
    parts = from_chips(block, chips)
    if after is None:
        return sum(part.astype(F32) for part in parts).astype(BF16)
    return add_parts(parts, after)


def in_vmem(block):
    return pltpu.with_memory_space_constraint(block, pltpu.VMEM)


def in_hbm(block):
    return pltpu.with_memory_space_constraint(block, pltpu.HBM)


def params(mib):
    return pltpu.CompilerParams(vmem_limit_bytes=mib * MIB)


def cost(flops, nbytes):
    return pl.CostEstimate(flops=flops, bytes_accessed=nbytes, transcendentals=0)


def turned(vector):
    count = vector.shape[0] // 2
    return jnp.concatenate([-vector[count:], vector[:count]], axis=0)


def operands(vector):
    return vector.astype(BF16), turned(vector).astype(BF16)


def times(vector, real_matrix, imag_matrix, contract):
    straight, cross = operands(vector)
    dims = (((1,), (contract,)), ((), ()))
    return lax.dot_general(
        straight, real_matrix, dims, preferred_element_type=F32
    ) + lax.dot_general(cross, imag_matrix, dims, preferred_element_type=F32)


def transpose_sep(sep, after):
    _, rows, total = sep.shape
    step = 128 if rows % 128 == 0 else rows
    chunks = [(part, at) for part in range(2) for at in range(0, rows, step)]

    def kernel(sep_ref, _, out, stored, done):
        copies = []
        for index, (part, at) in enumerate(chunks):
            piece = (part, pl.ds(at, step))
            copy = pltpu.make_async_copy(sep_ref.at[piece], stored.at[piece], done.at[index])
            copy.start()
            copies.append(copy)
        for copy, (part, at) in zip(copies, chunks):
            copy.wait()
            out[part, :, pl.ds(at, step)] = stored[part, pl.ds(at, step), :].T

    return pl.pallas_call(
        kernel,
        in_specs=[ANY, ANY],
        out_specs=VMEM,
        out_shape=pltpu.VMEM((2, total, rows), BF16),
        scratch_shapes=[pltpu.VMEM(sep.shape, BF16), pltpu.SemaphoreType.DMA((len(chunks),))],
        compiler_params=params(18),
        cost_estimate=cost(0, 4 * sep.size),
        name="transpose_sep",
    )(in_hbm(sep), after)


def hold(blocks, after):
    def kernel(*refs):
        del refs

    return pl.pallas_call(
        kernel,
        in_specs=[ANY] * (len(blocks) + 1),
        out_specs=[ANY] * len(blocks),
        out_shape=[jax.ShapeDtypeStruct(block.shape, block.dtype) for block in blocks],
        input_output_aliases={index: index for index in range(len(blocks))},
        compiler_params=params(1),
        name="hold",
    )(*blocks, after)


def transpose_gather(own, theirs, after):
    _, total, cells = own.shape
    half = total // 2
    step = 512

    def kernel(own_ref, theirs_ref, _, out):
        start = (lax.axis_index("front") % 2) * half
        for side, block in enumerate((own_ref, theirs_ref)):
            for part in range(2):
                for at in range(0, half, step):
                    rows = pl.ds(pl.multiple_of(start + at, step), step)
                    out[part, pl.ds(side * cells, cells), pl.ds(at, step)] = block[part, rows, :].T

    return pl.pallas_call(
        kernel,
        in_specs=[VMEM, VMEM, ANY],
        out_specs=VMEM,
        out_shape=pltpu.VMEM((2, 2 * cells, half), BF16),
        compiler_params=params(16),
        cost_estimate=cost(0, 4 * own.size),
        name="transpose_gather",
    )(in_vmem(own), in_vmem(theirs), after)


def panel_columns(owner_ref, step, rows):
    slots = owner_ref.shape[0]
    place = lax.axis_index("front")
    chips = slots // 2
    chip = place // 2 ^ ((chips - step) % chips) if chips <= FEW_CHIPS else step
    panel = jnp.int32(0)
    for at in range(1, slots):
        panel = jnp.where(owner_ref[at] == 2 * chip + place % 2, at, panel)
    return pl.ds(pl.multiple_of(panel * rows, 128), rows)


def transpose_maps(own, theirs, owner, rows, after):
    _, cells, width = own.shape
    slots = owner.shape[0]
    chips = slots // 2

    def kernel(owner_ref, own_ref, theirs_ref, _, out, blocks_out):
        for step in range(chips):
            columns = panel_columns(owner_ref, step, rows)
            for side, block in enumerate((own_ref, theirs_ref)):
                for part in range(2):
                    out[part, pl.ds(step * rows, rows), pl.ds(side * cells, cells)] = block[
                        part, :, columns
                    ].T
        for side, block in enumerate((own_ref, theirs_ref)):
            for kind in range(3):
                columns = pl.ds(slots * rows + kind * cells, cells)
                for part in range(2):
                    blocks_out[side, kind, part] = block[part, :, columns]

    return pl.pallas_call(
        kernel,
        in_specs=[SMEM, VMEM, VMEM, ANY],
        out_specs=[VMEM, VMEM],
        out_shape=[
            pltpu.VMEM((2, chips * rows, 2 * cells), BF16),
            jax.ShapeDtypeStruct((2, 3, 2, cells, cells), BF16),
        ],
        compiler_params=params(16),
        cost_estimate=cost(0, 4 * own.size),
        name="transpose_maps",
    )(owner, in_vmem(own), in_vmem(theirs), after)


def take_maps(own, theirs, owner, rows):
    _, cells, width = own.shape
    slots = owner.shape[0]
    total = slots * rows
    place = lax.axis_index("front")
    slot_ids = jnp.arange(slots, dtype=jnp.int32)
    panel_of = jnp.sum(jnp.where(owner[None, :] == slot_ids[:, None], slot_ids[None, :], 0), axis=1)
    wanted = panel_of[2 * arrival_order(place // 2, slots // 2) + place % 2]

    def columns(maps):
        chosen = jnp.take(maps[:, :, :total].reshape(2, cells, slots, rows), wanted, axis=2)
        return jnp.swapaxes(chosen.reshape(2, cells, total // 2), 1, 2)

    def blocks(maps):
        return jnp.moveaxis(maps[:, :, total:].reshape(2, cells, 3, cells), 2, 0)

    spread = jnp.concatenate([columns(own), columns(theirs)], axis=2)
    return spread, jnp.stack([blocks(own), blocks(theirs)])


def add_parts(parts, after):
    def kernel(*refs):
        out = refs[-1]
        total = refs[0][...].astype(F32)
        for part in refs[1 : len(parts)]:
            total = total + part[...].astype(F32)
        out[...] = total.astype(BF16)

    return pl.pallas_call(
        kernel,
        in_specs=[VMEM] * len(parts) + [ANY],
        out_specs=VMEM,
        out_shape=jax.ShapeDtypeStruct(parts[0].shape, BF16),
        compiler_params=params(16),
        cost_estimate=cost(4 * parts[0].size, 10 * parts[0].size),
        name="add_parts",
    )(*parts, in_vmem(after))


def join_parts(parts, after):
    width = parts[0].shape[1]

    def kernel(*refs):
        out = refs[-1]
        for index, part in enumerate(refs[: len(parts)]):
            out[:, pl.ds(index * width, width)] = part[...]

    return pl.pallas_call(
        kernel,
        in_specs=[VMEM] * len(parts) + [ANY],
        out_specs=VMEM,
        out_shape=jax.ShapeDtypeStruct((8, len(parts) * width), BF16),
        compiler_params=params(16),
        cost_estimate=cost(0, 8 * parts[0].size),
        name="join_parts",
    )(*parts, in_vmem(after))


def first_leaf_and_gather(sources, leaf, gather):
    cells = gather.shape[2]
    half = gather.shape[1] // 2

    def kernel(*refs):
        sources_hbm, leaf_hbm, gather_hbm, keep, give, gather_ref = refs[:6]
        sources_ref, leaf_ref, done = refs[6:]
        core = lax.axis_index("front") % 2
        layer = lax.axis_index("layer")
        sides = [pl.ds(pl.multiple_of(side * half, half), half) for side in (1 - core, core)]
        values_at, sources_at = pl.ds(half, cells), pl.ds(half + cells, cells)
        pieces = [(sources_hbm, sources_ref), (leaf_hbm, leaf_ref)]
        for rows in sides:
            for part in range(2):
                pieces.append((gather_hbm.at[part, rows], gather_ref.at[part, rows]))
        copies = [
            pltpu.make_async_copy(source, target, done.at[index])
            for index, (source, target) in enumerate(pieces)
        ]
        for copy in copies:
            copy.start()
        copies[0].wait()
        copies[1].wait()
        source = jnp.concatenate([sources_ref[0], sources_ref[1]], axis=0)
        for out in (give, keep):
            out[:, sources_at] = source

        @pl.when(layer == 0)
        def _():
            leaf_values = times(source, leaf_ref[0], leaf_ref[1], 1)
            for out in (give, keep):
                out[:, values_at] = leaf_values

        for index, (out, rows) in enumerate(zip((give, keep), sides)):
            copies[2 + 2 * index].wait()
            copies[3 + 2 * index].wait()

            @pl.when(layer == 0)
            def _(out=out, rows=rows):
                leaf_values = out[:, values_at]
                out[:, pl.ds(0, half)] = times(
                    leaf_values, gather_ref[0, rows, :], gather_ref[1, rows, :], 1
                )

    return pl.pallas_call(
        kernel,
        in_specs=[ANY] * 3,
        out_specs=[VMEM] * 3,
        out_shape=[
            jax.ShapeDtypeStruct((8, half + 2 * cells), F32),
            jax.ShapeDtypeStruct((8, half + 2 * cells), F32),
            pltpu.VMEM(gather.shape, BF16),
        ],
        scratch_shapes=[
            pltpu.VMEM(sources.shape, F32),
            pltpu.VMEM(leaf.shape, BF16),
            pltpu.SemaphoreType.DMA((6,)),
        ],
        compiler_params=params(16),
        cost_estimate=cost(16 * gather.size, 2 * gather.size),
        name="first_leaf_and_gather",
    )(in_hbm(sources), in_hbm(leaf), in_hbm(gather))


def load_maps(maps, after):
    widths = [block.shape[2] for block in maps]

    def kernel(*refs):
        out, done = refs[-2:]
        copies = []
        for index, width in enumerate(widths):
            columns = pl.ds(sum(widths[:index]), width)
            copies.append(
                pltpu.make_async_copy(refs[index], out.at[:, :, columns], done.at[index])
            )
        for copy in copies:
            copy.start()
        for copy in copies:
            copy.wait()

    return pl.pallas_call(
        kernel,
        in_specs=[ANY] * (len(maps) + 1),
        out_specs=VMEM,
        out_shape=pltpu.VMEM((*maps[0].shape[:2], sum(widths)), BF16),
        scratch_shapes=[pltpu.SemaphoreType.DMA((len(maps),))],
        compiler_params=params(16),
        cost_estimate=cost(0, 4 * maps[0].size),
        name="load_maps",
    )(*[in_hbm(block) for block in maps], after)


def leaf_and_gather(level, blocks, gather, arrived, sources=None):
    cells = blocks.shape[3]
    width = gather.shape[2]
    given = list(arrived) if sources is None else [*arrived, sources]

    def kernel(*refs):
        blocks_ref, gather_ref, leaf_out, sums_out = refs[-4:]

        def apply(vector, kind):
            return jnp.concatenate(
                [
                    times(
                        vector[:, side * cells : (side + 1) * cells],
                        blocks_ref[side, kind, 0],
                        blocks_ref[side, kind, 1],
                        1,
                    )
                    for side in range(2)
                ],
                axis=1,
            )

        @pl.when(lax.axis_index("layer") == level)
        def _():
            crossed = jnp.concatenate([refs[1][:, cells:], refs[1][:, :cells]], axis=1)
            source = apply(refs[0][...] + crossed, 2 if sources is None else 1)
            if sources is not None:
                source = refs[2][...] - source
            leaf_values = apply(source, 0)
            leaf_out[...] = leaf_values
            sums_out[...] = times(leaf_values, gather_ref[0], gather_ref[1], 0).astype(BF16)

    return pl.pallas_call(
        kernel,
        in_specs=[VMEM] * (len(given) + 2),
        out_specs=[VMEM, VMEM],
        out_shape=[
            jax.ShapeDtypeStruct((8, 2 * cells), F32),
            jax.ShapeDtypeStruct((8, width), BF16),
        ],
        compiler_params=params(16),
        cost_estimate=cost(32 * gather.size, 2 * gather.size),
        name="leaf_and_gather",
    )(*given, blocks, in_vmem(gather))


def folded(blocks, gather, kind, layers, after):
    cells = blocks.shape[3]

    def kernel(blocks_ref, gather_ref, _, out):
        layer = lax.axis_index("layer")

        @pl.when(jnp.logical_and(layer >= layers[0], layer <= layers[-1]))
        def _():
            for side in range(2):
                left = [blocks_ref[side, 0, part] for part in range(2)]
                right = [blocks_ref[side, kind, part] for part in range(2)]

                def product(i, j, left=left, right=right):
                    return jnp.dot(left[i], right[j], preferred_element_type=F32)

                real = (product(0, 0) - product(1, 1)).T
                imag = (product(0, 1) + product(1, 0)).T
                at = pl.ds(side * cells, cells)
                maps = [gather_ref[part, at, :] for part in range(2)]

                def applied(matrix, part, maps=maps):
                    return jnp.dot(matrix.astype(BF16), maps[part], preferred_element_type=F32)

                out[0, at, :] = (applied(real, 0) - applied(imag, 1)).astype(BF16)
                out[1, at, :] = (applied(real, 1) + applied(imag, 0)).astype(BF16)

    return pl.pallas_call(
        kernel,
        in_specs=[VMEM, VMEM, ANY],
        out_specs=VMEM,
        out_shape=pltpu.VMEM(gather.shape, BF16),
        compiler_params=params(20),
        cost_estimate=cost(8 * cells * gather.size, 4 * gather.size),
        name="folded",
    )(blocks, in_vmem(gather), after)


def block_products(vector, blocks_ref, kind):
    cells = blocks_ref.shape[3]
    return jnp.concatenate(
        [
            times(
                vector[:, side * cells : (side + 1) * cells],
                blocks_ref[side, kind, 0],
                blocks_ref[side, kind, 1],
                1,
            )
            for side in range(2)
        ],
        axis=1,
    )


def source_sums(blocks, gather, sources, layers):
    def kernel(blocks_ref, gather_ref, sources_ref, leaf_out, sums_out):
        layer = lax.axis_index("layer")

        @pl.when(jnp.logical_and(layer >= layers[0], layer <= layers[-1]))
        def _():
            leaf_values = block_products(sources_ref[...], blocks_ref, 0)
            leaf_out[...] = leaf_values
            sums_out[...] = times(leaf_values, gather_ref[0], gather_ref[1], 0)

    return pl.pallas_call(
        kernel,
        in_specs=[VMEM] * 3,
        out_specs=[VMEM] * 2,
        out_shape=[
            jax.ShapeDtypeStruct(sources.shape, F32),
            jax.ShapeDtypeStruct((8, gather.shape[2]), F32),
        ],
        compiler_params=params(16),
        cost_estimate=cost(32 * gather.size, 2 * gather.size),
        name="source_sums",
    )(blocks, in_vmem(gather), sources)


def folded_sums(level, arrived, fold, own_sums=None):
    given = [*arrived] if own_sums is None else [*arrived, own_sums]

    def kernel(*refs):
        fold_ref, out = refs[-2:]
        cells = refs[0].shape[1] // 2

        @pl.when(lax.axis_index("layer") == level)
        def _():
            crossed = jnp.concatenate([refs[1][:, cells:], refs[1][:, :cells]], axis=1)
            sums = times(refs[0][...] + crossed, fold_ref[0], fold_ref[1], 0)
            if own_sums is not None:
                sums = refs[2][...] - sums
            out[...] = sums.astype(BF16)

    return pl.pallas_call(
        kernel,
        in_specs=[VMEM] * (len(given) + 1),
        out_specs=VMEM,
        out_shape=jax.ShapeDtypeStruct((8, fold.shape[2]), BF16),
        compiler_params=params(16),
        cost_estimate=cost(32 * fold.size, 2 * fold.size),
        name="folded_sums",
    )(*given, in_vmem(fold))


def leaf_only(level, arrived, blocks, own_values=None):
    given = [*arrived] if own_values is None else [*arrived, own_values]

    def kernel(*refs):
        blocks_ref, out = refs[-2:]
        cells = blocks_ref.shape[3]

        @pl.when(lax.axis_index("layer") == level)
        def _():
            crossed = jnp.concatenate([refs[1][:, cells:], refs[1][:, :cells]], axis=1)
            kind = 2 if own_values is None else 1
            coupled = block_products(refs[0][...] + crossed, blocks_ref, kind)
            value = block_products(coupled, blocks_ref, 0)
            out[...] = value if own_values is None else refs[2][...] - value

    return pl.pallas_call(
        kernel,
        in_specs=[VMEM] * (len(given) + 1),
        out_specs=VMEM,
        out_shape=jax.ShapeDtypeStruct(arrived[0].shape, F32),
        compiler_params=params(16),
        cost_estimate=cost(16 * blocks.size, 2 * blocks.size),
        name="leaf_only",
    )(*given, blocks)


def sep_rows(level, sums, sep, other, before=None):
    half = sums.shape[1]
    rows = sep.shape[2]
    given = [sums] if before is None else [sums, before]

    def kernel(*refs):
        sums_ref, sep_ref, out = refs[0], refs[len(given)], refs[-1]

        @pl.when(lax.axis_index("layer") == level)
        def _():
            core = lax.axis_index("front") % 2
            side = 1 - core if other else core
            at = pl.ds(pl.multiple_of(side * half, half), half)
            value = times(sums_ref[...].astype(F32), sep_ref[0, at, :], sep_ref[1, at, :], 0)
            if before is not None:
                value = value + refs[1][...]
            out[...] = value.astype(out.dtype)

    return pl.pallas_call(
        kernel,
        in_specs=[VMEM] * (len(given) + 1),
        out_specs=VMEM,
        out_shape=jax.ShapeDtypeStruct((8, rows), F32 if before is None else BF16),
        compiler_params=params(16),
        cost_estimate=cost(16 * sep.size, sep.size),
        name="sep_rows",
    )(*given, in_vmem(sep))


def share_of_value(part, leaf_values, before, subtract):
    first = jnp.where(lax.axis_index("front") % 2 == 0, 1.0, 0.0)
    if subtract:
        return first * (before - leaf_values) + part
    return first * leaf_values - part


def spread_cells(level, stored, spread, leaf_values, held=(), before=None, last=False):
    given = [stored, leaf_values, *held] + ([] if before is None else [before])
    outputs = 2 if last else 3

    def kernel(*refs):
        stored_ref, leaf_ref = refs[:2]
        spread_ref = refs[len(given)]
        part_out, leaf_out = refs[len(given) + 1 : len(given) + 3]
        here = lax.axis_index("layer") == level

        @pl.when(here)
        def _():
            part = times(stored_ref[...].astype(F32), spread_ref[0], spread_ref[1], 0)
            part_out[...] = part
            leaf_out[...] = leaf_ref[...]
            if not last:
                value = None if before is None else refs[len(given) - 1][...]
                refs[-1][...] = share_of_value(part, leaf_ref[...], value, before is not None)

        if held:

            @pl.when(jnp.logical_not(here))
            def _():
                part_out[...] = refs[2][...]
                leaf_out[...] = refs[3][...]

    return pl.pallas_call(
        kernel,
        in_specs=[VMEM] * (len(given) + 1),
        out_specs=[VMEM] * outputs,
        out_shape=[jax.ShapeDtypeStruct((8, spread.shape[2]), F32)] * outputs,
        compiler_params=params(16),
        cost_estimate=cost(32 * spread.size, 2 * spread.size),
        name="spread_cells",
    )(*given, in_vmem(spread))


def finish(part, leaf_values, before=None, depth=0):
    cells = part.shape[1] // 2
    given = [leaf_values, part, pair(part)] + ([] if before is None else [before])

    def kernel(*refs):
        leaf_ref, part_ref, theirs_ref = refs[:3]
        swapped = jnp.concatenate([theirs_ref[:, cells:], theirs_ref[:, :cells]], axis=1)
        solved = leaf_ref[...] - (part_ref[...] + swapped)
        if before is None:
            refs[-1][...] = solved
        else:
            bottom = lax.axis_index("layer") == depth - 1
            value = refs[3][...] - jnp.where(bottom, 0.0, solved)
            refs[-1][0, 0] = value[:4, :cells]
            refs[-1][0, 1] = value[4:, :cells]

    return pl.pallas_call(
        kernel,
        in_specs=[VMEM] * len(given),
        out_specs=VMEM,
        out_shape=jax.ShapeDtypeStruct(part.shape if before is None else (1, 2, 4, cells), F32),
        compiler_params=params(16),
        cost_estimate=cost(4 * part.size, 16 * part.size),
        name="finish",
    )(*given)


def local(
    right_sides,
    leaf_inverse,
    couple_above,
    couple_below,
    sep_gather,
    sep_inverse,
    sep_spread,
    panel_owner,
):
    depth = lax.axis_size("layer")
    cells = leaf_inverse.shape[2]
    rows = sep_inverse.shape[2]

    maps = [sep_spread[0], leaf_inverse[0], couple_above[0], couple_below[0]]
    keep, give, own_gather = first_leaf_and_gather(right_sides[0], leaf_inverse[0], sep_gather[0])
    got = pair(give)
    own_maps = load_maps(maps, give)
    half = sep_gather.shape[2] // 2
    first_sums = (keep[:, :half] + got[:, :half]).astype(BF16)
    first_values, sources = (
        jnp.concatenate([block[:, at : at + cells] for block in (keep, got)], axis=1)
        for at in (half, half + cells)
    )

    own_gather, own_maps = hold([own_gather, own_maps], first_sums)
    their_gather, their_maps = pair(own_gather), pair(own_maps)
    sep = transpose_sep(sep_inverse[0], first_sums)

    def own_rows_of(level, half_sums):
        other_sums = pair(half_sums)
        own_rows = sep_rows(level, half_sums, sep, False)
        return sep_rows(level, other_sums, sep, True, own_rows)

    def solve(level, arrived, held, before=None, last=False):
        if before is not None:
            sums = folded_sums(level, arrived, fold_below)
            leaf_values = leaf_only(level, arrived, blocks)
        elif level > 1:
            sums = folded_sums(level, arrived, fold_above, source_parts[1])
            leaf_values = leaf_only(level, arrived, blocks, source_parts[0])
        else:
            leaf_values, sums = leaf_and_gather(level, blocks, gather, arrived, sources)
        stored = gather_chips(own_rows_of(level, sum_chips(sums, leaf_values)))
        return spread_cells(level, stored, spread, leaf_values, held, before, last)

    own_rows = own_rows_of(0, sum_chips(first_sums, sep))
    if rows % 128 == 0:
        spread, blocks = transpose_maps(own_maps, their_maps, panel_owner[0], rows, own_rows)
    else:
        spread, blocks = take_maps(own_maps, their_maps, panel_owner[0], rows)
    *held, share = spread_cells(0, gather_chips(own_rows, spread), spread, first_values)
    arrived = hop(share, 0, 1)
    gather = transpose_gather(own_gather, their_gather, share)

    fold_above = folded(blocks, gather, 1, range(2, depth), share)
    source_parts = source_sums(blocks, gather, sources, range(2, depth))

    for level in range(1, depth):
        if level > 1:
            arrived = hop(share, level - 1, level)
        *held, share = solve(level, arrived, held)
        if level == depth - 2:
            fold_below = folded(blocks, gather, 2, range(depth - 1), share)
    value = finish(*held)
    for level in range(depth - 2, 0, -1):
        arrived = hop(share, level + 1, level)
        *held, share = solve(level, arrived, held, value)
    held = solve(0, hop(share, 1, 0), held, value, last=True)
    return finish(*held, value, depth)


def solution(mesh):
    return jax.shard_map(
        local,
        mesh=mesh,
        in_specs=(
            P("layer", None, None, "front"),
            P("layer", None, "front", None),
            P("layer", None, "front", None),
            P("layer", None, "front", None),
            P("layer", None, None, "front"),
            P("layer", None, "front", None),
            P("layer", None, "front", None),
            P("layer", None),
        ),
        out_specs=P("layer", None, None, "front"),
        check_vma=False,
    )
```
